32 devices in a mesh: dp: 16 (over z, y, x), seq: 2 (over core).
Axes of the slice: x: 2, y: 2, z: 4, core: 2. Of those that a mesh axis runs over, the one named last changes fastest.
Arguments:
- acts: bfloat16 [4096, 4096], P('dp', 'seq'), may hold values from -6 to 6
- upstream: bfloat16 [4096, 1024], P(('dp', 'seq')), may hold values from -0.0234375 to 0.0234375
- keep_lists: int32 [64, 8], replicated, may hold values from 0 to 15, all different within a row
- left_gram: float32 [2, 16, 16, 64, 64], P('seq', 'dp'), as said below
- right_gram: float32 [2, 16, 16, 64, 64], P('seq', 'dp'), as said below
- left_basis: float32 [2, 16, 16, 64, 64], P('seq', 'dp'), may hold values from -0.75 to 0.75
- right_basis: float32 [2, 16, 16, 64, 64], P('seq', 'dp'), may hold values from -0.75 to 0.75
- second_moment: float32 [2, 16, 16, 64, 64], P('seq', 'dp'), may hold values from 0.004 to 0.04
Outputs:
- new_left: float32 [2, 16, 16, 64, 64], P('seq', 'dp')
- new_right: float32 [2, 16, 16, 64, 64], P('seq', 'dp')
- direction: float32 [2, 16, 16, 64, 64], P('seq', 'dp')
The draws below stay inside these ranges and needn't reach their ends.
Inputs may be any that keep to these rules, and one draw needn't show every extreme that they name: `keep_lists`: each row lists 8 different column blocks, and every column block is kept in some row. `left_gram`: each block is symmetric. `right_gram`: each block is symmetric.
All inputs are finite; a program needn't handle non-finite values.
Results may differ from the reference program's by a relative error of at most 0.0003.
Values may be sent and summed in bfloat16 or wider, within the bound.
A program may use at most 64 MiB of HBM per device.

```python
import math
import jax
import jax.numpy as jnp
from jax import lax

D = 4096
K_COLS = 1024
BLOCK = 64
ROW_BLOCKS = 64
COL_BLOCKS = 16
KEPT = 8
OWNED = 16
TOKENS = 4096
DP_SHARDS = 16
SEQ_SHARDS = 2


def gram_draw(key):
    noise = jax.random.normal(key, (SEQ_SHARDS, DP_SHARDS, OWNED, BLOCK, BLOCK), jnp.float32) * 0.2
    symmetric = 0.5 * (noise + jnp.swapaxes(noise, -1, -2))
    return symmetric + 0.5 * jnp.eye(BLOCK, dtype=jnp.float32)


def draw_left_gram(key, part):
    return gram_draw(jax.random.fold_in(key, 11))


def draw_right_gram(key, part):
    return gram_draw(jax.random.fold_in(key, 23))


def levels(rng, dims, split, low, largest):
    gain = 1.0
    for position, parts in split:
        heights = jax.random.uniform(jax.random.fold_in(jax.random.fold_in(rng, 6), position), (parts,), jnp.float32, low / len(split), largest / len(split))
        gain = gain * jnp.repeat(jnp.exp(heights), dims[position] // parts).reshape((-1,) + (1,) * (len(dims) - 1 - position))
    return gain


def picks_of(own_key, rows, count, top, lift):
    sequence = jax.random.permutation(jax.random.fold_in(own_key, 1), count)
    pull = sequence
    for power in range(3):
        pull = pull * pull // count
    pull = pull * lift // count
    tickets = jax.random.randint(jax.random.fold_in(own_key, 2), (rows, count), 0, 4096) + pull
    holders = jax.random.permutation(jax.random.fold_in(own_key, 3), rows)[jnp.arange(count) % rows]
    tickets = jnp.where(jnp.arange(rows)[:, None] == holders[None, :], 1 << 14, tickets)
    score = tickets * count + jnp.arange(count)
    return lax.top_k(score.astype(jnp.int32), top)[1].astype(jnp.int32)


def gaussian(key, dims, width, limit, split=(), kind=jnp.bfloat16):
    result = width * jax.random.normal(key, dims, jnp.float32)
    if split:
        result = result * levels(key, dims, split, -0.22, 0.18)
    return jnp.clip(result, -limit, limit).astype(kind)


def setup_inputs(seed: int = 0) -> dict:
    key_list = jax.random.split(jax.random.key(seed), 9)
    acts = gaussian(key_list[0], (TOKENS, D), 1.0, 6.0, ((0, 16), (1, 2)))
    upstream = gaussian(key_list[1], (TOKENS, K_COLS), (0.25 * TOKENS ** -0.5), 0.0234375, ((0, 32),))
    keep_lists = picks_of(key_list[2], ROW_BLOCKS, COL_BLOCKS, KEPT, 0)
    left_gram = draw_left_gram(jax.random.fold_in(key_list[8], 71), 0)
    right_gram = draw_right_gram(jax.random.fold_in(key_list[8], 71), 0)
    left_basis = gaussian(key_list[5], (SEQ_SHARDS, DP_SHARDS, OWNED, BLOCK, BLOCK), BLOCK ** -0.5, 0.75, ((0, 2), (1, 16)), jnp.float32)
    right_basis = gaussian(key_list[6], (SEQ_SHARDS, DP_SHARDS, OWNED, BLOCK, BLOCK), BLOCK ** -0.5, 0.75, ((0, 2), (1, 16)), jnp.float32)
    second_moment = jnp.clip(jnp.exp(math.log(0.04) - 2.30258502 * jax.random.uniform(key_list[7], (SEQ_SHARDS, DP_SHARDS, OWNED, BLOCK, BLOCK), jnp.float32) ** levels(key_list[7], (SEQ_SHARDS, DP_SHARDS, OWNED, BLOCK, BLOCK), ((0, 2), (1, 16)), -0.2, 0.2)), 0.004, 0.04)
    return {"acts": acts, "upstream": upstream, "keep_lists": keep_lists, "left_gram": left_gram, "right_gram": right_gram, "left_basis": left_basis, "right_basis": right_basis, "second_moment": second_moment}


def precondition(gradient, left_gram, right_gram, left_basis, right_basis, second_moment):
    highest = lax.Precision.HIGHEST
    new_left = 0.95 * left_gram + 0.05 * jnp.einsum('...ij,...kj->...ik', gradient, gradient, precision=highest)
    new_right = 0.95 * right_gram + 0.05 * jnp.einsum('...ji,...jk->...ik', gradient, gradient, precision=highest)
    partial_rot = jnp.einsum('...ji,...jk->...ik', left_basis, gradient, precision=highest)
    rotated = jnp.einsum('...ij,...jk->...ik', partial_rot, right_basis, precision=highest)
    second = 0.95 * second_moment + 0.05 * rotated * rotated
    scaled = rotated / (jnp.sqrt(second) + 1e-08)
    partial_back = jnp.einsum('...ij,...jk->...ik', left_basis, scaled, precision=highest)
    direction = jnp.einsum('...ij,...kj->...ik', partial_back, right_basis, precision=highest)
    return (new_left, new_right, direction)

def reference(acts, upstream, keep_lists, left_gram, right_gram, left_basis, right_basis, second_moment):
    grad = jnp.dot(acts.T, upstream, preferred_element_type=jnp.float32)
    tiles = grad.reshape(ROW_BLOCKS, BLOCK, COL_BLOCKS, BLOCK)
    picked = jnp.take_along_axis(tiles, keep_lists.astype(jnp.int32)[:, None, :, None], axis=2)
    blocks = picked.transpose(0, 2, 1, 3).reshape(SEQ_SHARDS, DP_SHARDS, OWNED, BLOCK, BLOCK)
    new_left, new_right, direction = precondition(blocks, left_gram, right_gram, left_basis, right_basis, second_moment)
    return (new_left, new_right, direction)
```

```python
import functools

import jax
import jax.numpy as jnp
from jax import lax
from jax.experimental import pallas as pl
from jax.experimental.pallas import tpu as pltpu
from jax.sharding import PartitionSpec as P

BLOCK = 64
LANES = 128
TOP = 32766.0
MESH = pl.DeviceIdType.MESH


def precondition(gradient, left_gram, right_gram, left_basis, right_basis, second_moment):
    highest = lax.Precision.HIGHEST
    new_left = 0.95 * left_gram + 0.05 * jnp.einsum(
        "...ij,...kj->...ik", gradient, gradient, precision=highest
    )
    new_right = 0.95 * right_gram + 0.05 * jnp.einsum(
        "...ji,...jk->...ik", gradient, gradient, precision=highest
    )
    partial_rot = jnp.einsum("...ji,...jk->...ik", left_basis, gradient, precision=highest)
    rotated = jnp.einsum("...ij,...jk->...ik", partial_rot, right_basis, precision=highest)
    second = 0.95 * second_moment + 0.05 * rotated * rotated
    scaled = rotated / (jnp.sqrt(second) + 1e-08)
    partial_back = jnp.einsum("...ij,...jk->...ik", left_basis, scaled, precision=highest)
    direction = jnp.einsum("...ij,...kj->...ik", partial_back, right_basis, precision=highest)
    return (new_left, new_right, direction)


def encode(value):
    peak = jnp.maximum(jnp.max(jnp.abs(value), axis=0, keepdims=True), 1e-30)
    coded = jnp.round(value * (TOP / peak)).astype(jnp.int32).astype(jnp.int16)
    return coded, peak * (1.0 / TOP)


def decode(coded, scale):
    return coded.astype(jnp.int32).astype(jnp.float32) * scale


def reduce_kernel(
    nz, kept, keep_ref, acts_ref, up_ref, out_ref,
    upt, product, acc,
    send1, send2, send3, recv1, recv2, recv3,
    ssend1, ssend2, ssend3, srecv1, srecv2, srecv3,
    up_sems, sems1, sems2, sems3,
):
    dp, seq = lax.axis_index("dp"), lax.axis_index("seq")
    x, y, z = lax.rem(dp, 2), lax.rem(dp // 2, 2), dp // 4
    ox, oy = 1 - x, 1 - y
    x_peer = (z * 2 + y) * 2 + ox
    y_peer = (z * 2 + oy) * 2 + x
    first_peer = (x_peer, y_peer)
    second_peer = (y_peer, x_peer)

    def z_peer(step):
        return (lax.rem(z + step + 1, nz) * 2 + y) * 2 + x

    barrier = pltpu.get_barrier_semaphore()
    pl.semaphore_signal(barrier, inc=1, device_id=(dp, 1 - seq), device_id_type=MESH)
    for peer in (x_peer, y_peer) + tuple(z_peer(step) for step in range(nz - 1)):
        pl.semaphore_signal(barrier, inc=1, device_id=(peer, seq), device_id_type=MESH)
    upt[seq] = up_ref[...].T
    pl.semaphore_wait(barrier, nz + 2)

    def remote(src, dst, sems, peer):
        return pltpu.make_async_remote_copy(
            src_ref=src, dst_ref=dst, send_sem=sems.at[0], recv_sem=sems.at[1],
            device_id=peer, device_id_type=MESH,
        )

    up_copy = remote(upt.at[seq], upt.at[seq], up_sems, (dp, 1 - seq))
    up_copy.start()
    up_copy.wait()

    half_slots = kept // 2
    half_rows = half_slots * BLOCK
    blocks = 2 * (acts_ref.shape[1] // LANES)
    low = lax.broadcasted_iota(jnp.int32, (BLOCK, LANES), 1) < BLOCK

    def copies1(half, step):
        peer = (first_peer[half], seq)
        return (
            remote(send1.at[half, step], recv1.at[half, step], sems1.at[half, step, 0], peer),
            remote(ssend1.at[half, step], srecv1.at[half, step], sems1.at[half, step, 1], peer),
        )

    def copies2(half, step):
        peer = (second_peer[half], seq)
        return (
            remote(send2.at[half, step], recv2.at[half, step], sems2.at[half, step, 0], peer),
            remote(ssend2.at[half, step], srecv2.at[half, step], sems2.at[half, step, 1], peer),
        )

    def copies3(half, step):
        peer = (z_peer(step), seq)
        return (
            remote(send3.at[half, step], recv3.at[half, step], sems3.at[half, step, 0], peer),
            remote(ssend3.at[half, step], srecv3.at[half, step], sems3.at[half, step, 1], peer),
        )

    def produce(step, carry):
        to_z = lax.rem(z + step + 1, nz)
        for dy in range(2):
            base = (to_z * 2 + (y if dy == 0 else oy)) * 2
            columns = pl.ds(pl.multiple_of(base * LANES, 2 * LANES), 2 * LANES)
            whole = jnp.dot(
                jnp.concatenate([upt[0], upt[1]], axis=1),
                acts_ref[:, columns],
                preferred_element_type=jnp.float32,
            )
            product[0] = whole[:, :LANES].reshape(-1, BLOCK, LANES)
            product[1] = whole[:, LANES:].reshape(-1, BLOCK, LANES)
            for dx in range(2):
                to_x = x if dx == 0 else ox
                row_block = seq * blocks + (base + to_x) * 2
                for half in range(2):
                    parts = []
                    for slot in range(half * half_slots, (half + 1) * half_slots):
                        top = keep_ref[row_block * kept + slot]
                        bottom = keep_ref[(row_block + 1) * kept + slot]
                        parts.append(
                            jnp.where(low, product[to_x, top], product[to_x, bottom])
                        )
                    value = jnp.concatenate(parts, axis=0)
                    away, slot = ((dx, dy), (dy, dx))[half]
                    if away:
                        coded, scale = encode(value)
                        send1[half, step, slot] = coded
                        ssend1[half, step, slot] = jnp.broadcast_to(scale, (8, LANES))
                    else:
                        acc[half, step, slot] = value
        for half in range(2):
            for copy in copies1(half, step):
                copy.start()
        return carry

    lax.fori_loop(0, nz, produce, 0)

    for step in range(nz + 1):
        if step < nz:
            for half in range(2):
                for copy in copies1(half, step):
                    copy.wait_recv()
                away = acc[half, step, 1] + decode(
                    recv1[half, step, 1], srecv1[half, step, 1, 0:1, :]
                )
                coded, scale = encode(away)
                send2[half, step] = coded
                ssend2[half, step] = jnp.broadcast_to(scale, (8, LANES))
                for copy in copies2(half, step):
                    copy.start()
                acc[half, step, 0] += decode(
                    recv1[half, step, 0], srecv1[half, step, 0, 0:1, :]
                )
        if step > 0:
            done = step - 1
            for half in range(2):
                for copy in copies2(half, done):
                    copy.wait_recv()
                total = acc[half, done, 0] + decode(
                    recv2[half, done], srecv2[half, done, 0:1, :]
                )
                if done < nz - 1:
                    coded, scale = encode(total)
                    send3[half, done] = coded
                    ssend3[half, done] = jnp.broadcast_to(scale, (8, LANES))
                    for copy in copies3(half, done):
                        copy.start()
                else:
                    acc[half, done, 0] = total

    for half in range(2):
        total = acc[half, nz - 1, 0]
        for step in range(nz - 1):
            for copy in copies3(half, step):
                copy.wait_recv()
            total += decode(recv3[half, step], srecv3[half, step, 0:1, :])
        out_ref[half * half_rows : (half + 1) * half_rows, :] = total

    for half in range(2):
        for step in range(nz):
            for copy in copies1(half, step) + copies2(half, step):
                copy.wait_send()
            if step < nz - 1:
                for copy in copies3(half, step):
                    copy.wait_send()


def reduced_blocks(acts, upstream, keep_lists, nz):
    kept = keep_lists.shape[1]
    half_rows = kept // 2 * BLOCK
    tokens, rows = upstream.shape[0], upstream.shape[1]
    rest = max(nz - 1, 1)
    half = (half_rows, LANES)
    scale = (8, LANES)
    dma = pltpu.SemaphoreType.DMA
    vmem = pl.BlockSpec(memory_space=pltpu.VMEM)
    return pl.pallas_call(
        functools.partial(reduce_kernel, nz, kept),
        out_shape=jax.ShapeDtypeStruct((kept * BLOCK, LANES), jnp.float32),
        in_specs=[pl.BlockSpec(memory_space=pltpu.SMEM), vmem, vmem],
        out_specs=vmem,
        scratch_shapes=[
            pltpu.VMEM((2, rows, tokens), jnp.bfloat16),
            pltpu.VMEM((2, rows // BLOCK, BLOCK, LANES), jnp.float32),
            pltpu.VMEM((2, nz, 2) + half, jnp.float32),
            pltpu.VMEM((2, nz, 2) + half, jnp.int16),
            pltpu.VMEM((2, nz) + half, jnp.int16),
            pltpu.VMEM((2, rest) + half, jnp.int16),
            pltpu.VMEM((2, nz, 2) + half, jnp.int16),
            pltpu.VMEM((2, nz) + half, jnp.int16),
            pltpu.VMEM((2, rest) + half, jnp.int16),
            pltpu.VMEM((2, nz, 2) + scale, jnp.float32),
            pltpu.VMEM((2, nz) + scale, jnp.float32),
            pltpu.VMEM((2, rest) + scale, jnp.float32),
            pltpu.VMEM((2, nz, 2) + scale, jnp.float32),
            pltpu.VMEM((2, nz) + scale, jnp.float32),
            pltpu.VMEM((2, rest) + scale, jnp.float32),
            dma((2,)),
            dma((2, nz, 2, 2)),
            dma((2, nz, 2, 2)),
            dma((2, rest, 2, 2)),
        ],
        compiler_params=pltpu.CompilerParams(
            collective_id=0, has_side_effects=True, vmem_limit_bytes=48 * 1024 * 1024
        ),
        name="reduce_kept",
    )(keep_lists.reshape(-1), acts, upstream)


def per_device(
    acts, upstream, keep_lists, left_gram, right_gram, left_basis, right_basis, second_moment
):
    share_rows = acts.shape[1]
    share_blocks = share_rows // BLOCK
    kept = keep_lists.shape[1]
    data_size = lax.axis_size("dp")
    fits = (
        lax.axis_size("seq") == 2
        and data_size % 4 == 0
        and share_rows == data_size * LANES
        and kept % 2 == 0
        and upstream.shape[0] % LANES == 0
    )
    if fits:
        arrived = reduced_blocks(acts, upstream, keep_lists, data_size // 4)
        tiles = arrived.reshape(kept, BLOCK, LANES // BLOCK, BLOCK)
        gradient = tiles.transpose(2, 0, 3, 1).reshape(1, 1, -1, BLOCK, BLOCK)
    else:
        kept_share = lax.dynamic_slice_in_dim(
            keep_lists, lax.axis_index("seq") * share_blocks, share_blocks, 0
        )
        gathered = lax.all_gather(upstream, "seq", axis=0, tiled=True)
        grad = lax.dot_general(
            acts, gathered, (((0,), (0,)), ((), ())), preferred_element_type=jnp.float32
        )
        tiles = grad.reshape(share_blocks, BLOCK, grad.shape[1] // BLOCK, BLOCK)
        picked = jnp.take_along_axis(tiles, kept_share[:, None, :, None], axis=2)
        outgoing = picked.transpose(0, 2, 1, 3).reshape(data_size, -1, BLOCK * BLOCK)
        owned_sum = lax.psum_scatter(outgoing, "dp", scatter_dimension=0)
        gradient = owned_sum.reshape(1, 1, -1, BLOCK, BLOCK)
    return precondition(
        gradient, left_gram, right_gram, left_basis, right_basis, second_moment
    )


def solution(mesh):
    block = P("seq", "dp", None, None, None)
    return jax.shard_map(
        per_device,
        mesh=mesh,
        in_specs=(P("dp", "seq"), P(("dp", "seq"), None), P()) + (block,) * 5,
        out_specs=(block,) * 3,
        check_vma=False,
    )
```

```python
import functools

import jax
import jax.numpy as jnp
from jax import lax
from jax.experimental import pallas as pl
from jax.experimental.pallas import tpu as pltpu
from jax.sharding import PartitionSpec as P

BLOCK = 64
LANES = 128
TOP = 32766.0
MESH = pl.DeviceIdType.MESH


def precondition(gradient, left_gram, right_gram, left_basis, right_basis, second_moment):
    highest = lax.Precision.HIGHEST
    new_left = 0.95 * left_gram + 0.05 * jnp.einsum(
        "...ij,...kj->...ik", gradient, gradient, precision=highest
    )
    new_right = 0.95 * right_gram + 0.05 * jnp.einsum(
        "...ji,...jk->...ik", gradient, gradient, precision=highest
    )
    partial_rot = jnp.einsum("...ji,...jk->...ik", left_basis, gradient, precision=highest)
    rotated = jnp.einsum("...ij,...jk->...ik", partial_rot, right_basis, precision=highest)
    second = 0.95 * second_moment + 0.05 * rotated * rotated
    scaled = rotated / (jnp.sqrt(second) + 1e-08)
    partial_back = jnp.einsum("...ij,...jk->...ik", left_basis, scaled, precision=highest)
    direction = jnp.einsum("...ij,...kj->...ik", partial_back, right_basis, precision=highest)
    return (new_left, new_right, direction)


def encode(value):
    peak = jnp.maximum(jnp.max(jnp.abs(value), axis=0, keepdims=True), 1e-30)
    coded = jnp.round(value * (TOP / peak)).astype(jnp.int32).astype(jnp.int16)
    return coded, peak * (1.0 / TOP)


def decode(coded, scale):
    return coded.astype(jnp.int32).astype(jnp.float32) * scale


def reduce_kernel(
    nz, kept, keep_ref, acts_hbm, up_hbm, out_ref,
    acts, up, upt, product, acc,
    send1, send2, send3, recv1, recv2, recv3,
    ssend1, ssend2, ssend3, srecv1, srecv2, srecv3,
    load_sems, up_sems, sems1, sems2, sems3,
):
    dp, seq = lax.axis_index("dp"), lax.axis_index("seq")
    x, y, z = lax.rem(dp, 2), lax.rem(dp // 2, 2), dp // 4
    ox, oy = 1 - x, 1 - y
    x_peer = (z * 2 + y) * 2 + ox
    y_peer = (z * 2 + oy) * 2 + x
    first_peer = (x_peer, y_peer)
    second_peer = (y_peer, x_peer)

    def z_target(step):
        last = step // max(nz - 1, 1)
        return lax.rem(z + (1 - last) * (lax.rem(step + nz // 2 - 1, max(nz - 1, 1)) + 1), nz)

    def z_peer(step):
        return (z_target(step) * 2 + y) * 2 + x

    width = 4 * LANES

    def load(step):
        columns = pl.ds(pl.multiple_of(z_target(step) * width, width), width)
        return pltpu.make_async_copy(
            acts_hbm.at[:, columns], acts.at[step], load_sems.at[step + 1]
        )

    up_load = pltpu.make_async_copy(up_hbm, up, load_sems.at[0])
    up_load.start()
    for step in range(nz):
        load(step).start()

    barrier = pltpu.get_barrier_semaphore()
    pl.semaphore_signal(barrier, inc=1, device_id=(dp, 1 - seq), device_id_type=MESH)
    for peer in (x_peer, y_peer) + tuple(z_peer(step) for step in range(nz - 1)):
        pl.semaphore_signal(barrier, inc=1, device_id=(peer, seq), device_id_type=MESH)
    up_load.wait()
    upt[seq] = up[...].T
    pl.semaphore_wait(barrier, nz + 2)

    def remote(src, dst, sems, peer):
        return pltpu.make_async_remote_copy(
            src_ref=src, dst_ref=dst, send_sem=sems.at[0], recv_sem=sems.at[1],
            device_id=peer, device_id_type=MESH,
        )

    up_copy = remote(upt.at[seq], upt.at[seq], up_sems, (dp, 1 - seq))
    up_copy.start()
    up_copy.wait()

    half_slots = kept // 2
    half_rows = half_slots * BLOCK
    blocks = 8 * nz
    low = lax.broadcasted_iota(jnp.int32, (BLOCK, LANES), 1) < BLOCK

    def copies1(half, step):
        peer = (first_peer[half], seq)
        return (
            remote(send1.at[half, step], recv1.at[half, step], sems1.at[half, step, 0], peer),
            remote(ssend1.at[half, step], srecv1.at[half, step], sems1.at[half, step, 1], peer),
        )

    def copies2(half, step):
        peer = (second_peer[half], seq)
        return (
            remote(send2.at[half, step], recv2.at[half, step], sems2.at[half, step, 0], peer),
            remote(ssend2.at[half, step], srecv2.at[half, step], sems2.at[half, step, 1], peer),
        )

    def copies3(half, step):
        peer = (z_peer(step), seq)
        return (
            remote(send3.at[half, step], recv3.at[half, step], sems3.at[half, step, 0], peer),
            remote(ssend3.at[half, step], srecv3.at[half, step], sems3.at[half, step, 1], peer),
        )

    def produce(step):
        load(step).wait()
        for dy in (1, 0):
            to_y = y if dy == 0 else oy
            columns = pl.ds(pl.multiple_of(to_y * (2 * LANES), 2 * LANES), 2 * LANES)
            whole = jnp.dot(
                jnp.concatenate([upt[0], upt[1]], axis=1),
                acts[step, :, columns],
                preferred_element_type=jnp.float32,
            )
            product[0] = whole[:, :LANES].reshape(-1, BLOCK, LANES)
            product[1] = whole[:, LANES:].reshape(-1, BLOCK, LANES)
            for dx in (1, 0):
                to_x = x if dx == 0 else ox
                row_block = seq * blocks + ((z_target(step) * 2 + to_y) * 2 + to_x) * 2
                for half in range(2):
                    parts = []
                    for slot in range(half * half_slots, (half + 1) * half_slots):
                        top = keep_ref[row_block, slot]
                        bottom = keep_ref[row_block + 1, slot]
                        parts.append(
                            jnp.where(low, product[to_x, top], product[to_x, bottom])
                        )
                    value = jnp.concatenate(parts, axis=0)
                    away, slot = ((dx, dy), (dy, dx))[half]
                    if away:
                        coded, scale = encode(value)
                        send1[half, step, slot] = coded
                        ssend1[half, step, slot] = jnp.broadcast_to(scale, (8, LANES))
                    else:
                        acc[half, step, slot] = value
            for copy in copies1(dy, step):
                copy.start()

    def forward(step):
        for half in (1, 0):
            for copy in copies1(half, step):
                copy.wait_recv()
            away = acc[half, step, 1] + decode(
                recv1[half, step, 1], srecv1[half, step, 1, 0:1, :]
            )
            coded, scale = encode(away)
            send2[half, step] = coded
            ssend2[half, step] = jnp.broadcast_to(scale, (8, LANES))
            for copy in copies2(half, step):
                copy.start()
            acc[half, step, 0] += decode(recv1[half, step, 0], srecv1[half, step, 0, 0:1, :])

    def settle(step, half):
        for copy in copies2(half, step):
            copy.wait_recv()
        return acc[half, step, 0] + decode(recv2[half, step], srecv2[half, step, 0:1, :])

    def spread(step):
        for half in (1, 0):
            coded, scale = encode(settle(step, half))
            send3[half, step] = coded
            ssend3[half, step] = jnp.broadcast_to(scale, (8, LANES))
            for copy in copies3(half, step):
                copy.start()

    def turn(step, carry):
        @pl.when(step < nz)
        def _():
            produce(step)

        @pl.when((step >= 1) & (step <= nz))
        def _():
            forward(step - 1)

        @pl.when(step >= 2)
        def _():
            spread(step - 2)

        return carry

    lax.fori_loop(0, nz + 1, turn, 0)

    for half in range(2):
        total = settle(nz - 1, half)
        for step in range(nz - 1):
            for copy in copies3(half, step):
                copy.wait_recv()
            total += decode(recv3[half, step], srecv3[half, step, 0:1, :])
        out_ref[half * half_rows : (half + 1) * half_rows, :] = total

    for half in range(2):
        for step in range(nz):
            for copy in copies1(half, step) + copies2(half, step):
                copy.wait_send()
            if step < nz - 1:
                for copy in copies3(half, step):
                    copy.wait_send()


def reduced_blocks(acts, upstream, keep_lists, nz):
    kept = keep_lists.shape[1]
    half_rows = kept // 2 * BLOCK
    tokens, rows = upstream.shape[0], upstream.shape[1]
    rest = max(nz - 1, 1)
    half = (half_rows, LANES)
    scale = (8, LANES)
    dma = pltpu.SemaphoreType.DMA
    vmem, hbm = (pl.BlockSpec(memory_space=space) for space in (pltpu.VMEM, pl.ANY))
    return pl.pallas_call(
        functools.partial(reduce_kernel, nz, kept),
        out_shape=jax.ShapeDtypeStruct((kept * BLOCK, LANES), jnp.float32),
        in_specs=[pl.BlockSpec(memory_space=pltpu.SMEM), hbm, hbm],
        out_specs=vmem,
        scratch_shapes=[
            pltpu.VMEM((nz, acts.shape[0], 4 * LANES), jnp.bfloat16),
            pltpu.VMEM(upstream.shape, jnp.bfloat16),
            pltpu.VMEM((2, rows, tokens), jnp.bfloat16),
            pltpu.VMEM((2, rows // BLOCK, BLOCK, LANES), jnp.float32),
            pltpu.VMEM((2, nz, 2) + half, jnp.float32),
            pltpu.VMEM((2, nz, 2) + half, jnp.int16),
            pltpu.VMEM((2, nz) + half, jnp.int16),
            pltpu.VMEM((2, rest) + half, jnp.int16),
            pltpu.VMEM((2, nz, 2) + half, jnp.int16),
            pltpu.VMEM((2, nz) + half, jnp.int16),
            pltpu.VMEM((2, rest) + half, jnp.int16),
            pltpu.VMEM((2, nz, 2) + scale, jnp.float32),
            pltpu.VMEM((2, nz) + scale, jnp.float32),
            pltpu.VMEM((2, rest) + scale, jnp.float32),
            pltpu.VMEM((2, nz, 2) + scale, jnp.float32),
            pltpu.VMEM((2, nz) + scale, jnp.float32),
            pltpu.VMEM((2, rest) + scale, jnp.float32),
            dma((nz + 1,)),
            dma((2,)),
            dma((2, nz, 2, 2)),
            dma((2, nz, 2, 2)),
            dma((2, rest, 2, 2)),
        ],
        compiler_params=pltpu.CompilerParams(
            collective_id=0, has_side_effects=True, vmem_limit_bytes=24 * 1024 * 1024
        ),
        name="reduce_kept",
    )(keep_lists, acts, upstream)


def per_device(
    acts, upstream, keep_lists, left_gram, right_gram, left_basis, right_basis, second_moment
):
    share_rows = acts.shape[1]
    share_blocks = share_rows // BLOCK
    kept = keep_lists.shape[1]
    data_size = lax.axis_size("dp")
    fits = (
        lax.axis_size("seq") == 2
        and data_size % 4 == 0
        and share_rows == data_size * LANES
        and kept % 2 == 0
        and upstream.shape[0] % LANES == 0
    )
    if fits:
        arrived = reduced_blocks(acts, upstream, keep_lists, data_size // 4)
        tiles = arrived.reshape(kept, BLOCK, LANES // BLOCK, BLOCK)
        gradient = tiles.transpose(2, 0, 3, 1).reshape(1, 1, -1, BLOCK, BLOCK)
    else:
        kept_share = lax.dynamic_slice_in_dim(
            keep_lists, lax.axis_index("seq") * share_blocks, share_blocks, 0
        )
        gathered = lax.all_gather(upstream, "seq", axis=0, tiled=True)
        grad = lax.dot_general(
            acts, gathered, (((0,), (0,)), ((), ())), preferred_element_type=jnp.float32
        )
        tiles = grad.reshape(share_blocks, BLOCK, grad.shape[1] // BLOCK, BLOCK)
        picked = jnp.take_along_axis(tiles, kept_share[:, None, :, None], axis=2)
        outgoing = picked.transpose(0, 2, 1, 3).reshape(data_size, -1, BLOCK * BLOCK)
        owned_sum = lax.psum_scatter(outgoing, "dp", scatter_dimension=0)
        gradient = owned_sum.reshape(1, 1, -1, BLOCK, BLOCK)
    return precondition(
        gradient, left_gram, right_gram, left_basis, right_basis, second_moment
    )


def solution(mesh):
    block = P("seq", "dp", None, None, None)
    return jax.shard_map(
        per_device,
        mesh=mesh,
        in_specs=(P("dp", "seq"), P(("dp", "seq"), None), P()) + (block,) * 5,
        out_specs=(block,) * 3,
        check_vma=False,
    )
```

```python
import functools

import jax
import jax.numpy as jnp
from jax import lax
from jax.experimental import pallas as pl
from jax.experimental.pallas import tpu as pltpu
from jax.sharding import PartitionSpec as P

BLOCK = 64
LANES = 128
TOP = 32766.0
MESH = pl.DeviceIdType.MESH


def precondition(gradient, left_gram, right_gram, left_basis, right_basis, second_moment):
    highest = lax.Precision.HIGHEST
    new_left = 0.95 * left_gram + 0.05 * jnp.einsum(
        "...ij,...kj->...ik", gradient, gradient, precision=highest
    )
    new_right = 0.95 * right_gram + 0.05 * jnp.einsum(
        "...ji,...jk->...ik", gradient, gradient, precision=highest
    )
    partial_rot = jnp.einsum("...ji,...jk->...ik", left_basis, gradient, precision=highest)
    rotated = jnp.einsum("...ij,...jk->...ik", partial_rot, right_basis, precision=highest)
    second = 0.95 * second_moment + 0.05 * rotated * rotated
    scaled = rotated / (jnp.sqrt(second) + 1e-08)
    partial_back = jnp.einsum("...ij,...jk->...ik", left_basis, scaled, precision=highest)
    direction = jnp.einsum("...ij,...kj->...ik", partial_back, right_basis, precision=highest)
    return (new_left, new_right, direction)


def encode(value):
    peak = jnp.maximum(jnp.max(jnp.abs(value), axis=0, keepdims=True), 1e-30)
    coded = jnp.round(value * (TOP / peak)).astype(jnp.int32).astype(jnp.int16)
    return coded, peak * (1.0 / TOP)


def decode(coded, scale):
    return coded.astype(jnp.int32).astype(jnp.float32) * scale


def reduce_kernel(
    nz, kept, keep_ref, acts_hbm, up_hbm, out_ref,
    acts, up, upt, product, acc,
    send1, send2, send3, recv1, recv2, recv3,
    ssend1, ssend2, ssend3, srecv1, srecv2, srecv3,
    load_sems, up_sems, sems1, sems2, sems3,
):
    dp, seq = lax.axis_index("dp"), lax.axis_index("seq")
    x, y, z = lax.rem(dp, 2), lax.rem(dp // 2, 2), dp // 4
    ox, oy = 1 - x, 1 - y
    x_peer = (z * 2 + y) * 2 + ox
    y_peer = (z * 2 + oy) * 2 + x
    first_peer = (x_peer, y_peer)
    second_peer = (y_peer, x_peer)

    def z_target(step):
        last = step // max(nz - 1, 1)
        return lax.rem(z + (1 - last) * (lax.rem(step + nz // 2 - 1, max(nz - 1, 1)) + 1), nz)

    def z_peer(step):
        return (z_target(step) * 2 + y) * 2 + x

    width = 4 * LANES

    def load(step):
        columns = pl.ds(pl.multiple_of(z_target(step) * width, width), width)
        return pltpu.make_async_copy(
            acts_hbm.at[:, columns], acts.at[step], load_sems.at[step + 1]
        )

    up_load = pltpu.make_async_copy(up_hbm, up, load_sems.at[0])
    up_load.start()
    for step in range(nz):
        load(step).start()

    barrier = pltpu.get_barrier_semaphore()
    pl.semaphore_signal(barrier, inc=1, device_id=(dp, 1 - seq), device_id_type=MESH)
    for peer in (x_peer, y_peer) + tuple(z_peer(step) for step in range(nz - 1)):
        pl.semaphore_signal(barrier, inc=1, device_id=(peer, seq), device_id_type=MESH)
    up_load.wait()
    upt[seq] = up[...].T
    pl.semaphore_wait(barrier, nz + 2)

    def remote(src, dst, sems, peer):
        return pltpu.make_async_remote_copy(
            src_ref=src, dst_ref=dst, send_sem=sems.at[0], recv_sem=sems.at[1],
            device_id=peer, device_id_type=MESH,
        )

    up_copy = remote(upt.at[seq], upt.at[seq], up_sems, (dp, 1 - seq))
    up_copy.start()
    up_copy.wait()

    half_slots = kept // 2
    half_rows = half_slots * BLOCK
    blocks = 8 * nz
    low = lax.broadcasted_iota(jnp.int32, (BLOCK, LANES), 1) < BLOCK

    def copies1(half, step):
        peer = (first_peer[half], seq)
        return (
            remote(send1.at[half, step], recv1.at[half, step], sems1.at[half, step, 0], peer),
            remote(ssend1.at[half, step], srecv1.at[half, step], sems1.at[half, step, 1], peer),
        )

    def copies2(half, step):
        peer = (second_peer[half], seq)
        return (
            remote(send2.at[half, step], recv2.at[half, step], sems2.at[half, step, 0], peer),
            remote(ssend2.at[half, step], srecv2.at[half, step], sems2.at[half, step, 1], peer),
        )

    def copies3(half, step):
        peer = (z_peer(step), seq)
        return (
            remote(send3.at[half, step], recv3.at[half, step], sems3.at[half, step, 0], peer),
            remote(ssend3.at[half, step], srecv3.at[half, step], sems3.at[half, step, 1], peer),
        )

    def produce(step):
        load(step).wait()
        for dy in (1, 0):
            to_y = y if dy == 0 else oy
            columns = pl.ds(pl.multiple_of(to_y * (2 * LANES), 2 * LANES), 2 * LANES)
            whole = jnp.dot(
                jnp.concatenate([upt[0], upt[1]], axis=1),
                acts[step, :, columns],
                preferred_element_type=jnp.float32,
            )
            product[0] = whole[:, :LANES].reshape(-1, BLOCK, LANES)
            product[1] = whole[:, LANES:].reshape(-1, BLOCK, LANES)
            for dx in (1, 0):
                to_x = x if dx == 0 else ox
                row_block = seq * blocks + ((z_target(step) * 2 + to_y) * 2 + to_x) * 2
                for half in range(2):
                    parts = []
                    for slot in range(half * half_slots, (half + 1) * half_slots):
                        top = keep_ref[slot, row_block]
                        bottom = keep_ref[slot, row_block + 1]
                        parts.append(
                            jnp.where(low, product[to_x, top], product[to_x, bottom])
                        )
                    value = jnp.concatenate(parts, axis=0)
                    away, slot = ((dx, dy), (dy, dx))[half]
                    if away:
                        coded, scale = encode(value)
                        send1[half, step, slot] = coded
                        ssend1[half, step, slot] = jnp.broadcast_to(scale, (8, LANES))
                    else:
                        acc[half, step, slot] = value
            for copy in copies1(dy, step):
                copy.start()

    def forward(step):
        for half in (1, 0):
            for copy in copies1(half, step):
                copy.wait_recv()
            away = acc[half, step, 1] + decode(
                recv1[half, step, 1], srecv1[half, step, 1, 0:1, :]
            )
            coded, scale = encode(away)
            send2[half, step] = coded
            ssend2[half, step] = jnp.broadcast_to(scale, (8, LANES))
            for copy in copies2(half, step):
                copy.start()
            acc[half, step, 0] += decode(recv1[half, step, 0], srecv1[half, step, 0, 0:1, :])

    def settle(step, half):
        for copy in copies2(half, step):
            copy.wait_recv()
        return acc[half, step, 0] + decode(recv2[half, step], srecv2[half, step, 0:1, :])

    def spread(step):
        for half in (1, 0):
            coded, scale = encode(settle(step, half))
            send3[half, step] = coded
            ssend3[half, step] = jnp.broadcast_to(scale, (8, LANES))
            for copy in copies3(half, step):
                copy.start()

    def turn(step, carry):
        @pl.when(step < nz)
        def _():
            produce(step)

        @pl.when((step >= 1) & (step <= nz))
        def _():
            forward(step - 1)

        @pl.when(step >= 2)
        def _():
            spread(step - 2)

        return carry

    lax.fori_loop(0, nz + 1, turn, 0)

    for half in range(2):
        total = settle(nz - 1, half)
        for step in range(nz - 1):
            for copy in copies3(half, step):
                copy.wait_recv()
            total += decode(recv3[half, step], srecv3[half, step, 0:1, :])
        out_ref[half * half_rows : (half + 1) * half_rows, :] = total

    for half in range(2):
        for step in range(nz):
            for copy in copies1(half, step) + copies2(half, step):
                copy.wait_send()
            if step < nz - 1:
                for copy in copies3(half, step):
                    copy.wait_send()


def reduced_blocks(acts, upstream, keep_lists, nz):
    kept = keep_lists.shape[1]
    half_rows = kept // 2 * BLOCK
    tokens, rows = upstream.shape[0], upstream.shape[1]
    rest = max(nz - 1, 1)
    half = (half_rows, LANES)
    scale = (8, LANES)
    dma = pltpu.SemaphoreType.DMA
    vmem, hbm = (pl.BlockSpec(memory_space=space) for space in (pltpu.VMEM, pltpu.HBM))
    return pl.pallas_call(
        functools.partial(reduce_kernel, nz, kept),
        out_shape=jax.ShapeDtypeStruct((kept * BLOCK, LANES), jnp.float32),
        in_specs=[pl.BlockSpec(memory_space=pltpu.SMEM), hbm, hbm],
        out_specs=vmem,
        scratch_shapes=[
            pltpu.VMEM((nz, acts.shape[0], 4 * LANES), jnp.bfloat16),
            pltpu.VMEM(upstream.shape, jnp.bfloat16),
            pltpu.VMEM((2, rows, tokens), jnp.bfloat16),
            pltpu.VMEM((2, rows // BLOCK, BLOCK, LANES), jnp.float32),
            pltpu.VMEM((2, nz, 2) + half, jnp.float32),
            pltpu.VMEM((2, nz, 2) + half, jnp.int16),
            pltpu.VMEM((2, nz) + half, jnp.int16),
            pltpu.VMEM((2, rest) + half, jnp.int16),
            pltpu.VMEM((2, nz, 2) + half, jnp.int16),
            pltpu.VMEM((2, nz) + half, jnp.int16),
            pltpu.VMEM((2, rest) + half, jnp.int16),
            pltpu.VMEM((2, nz, 2) + scale, jnp.float32),
            pltpu.VMEM((2, nz) + scale, jnp.float32),
            pltpu.VMEM((2, rest) + scale, jnp.float32),
            pltpu.VMEM((2, nz, 2) + scale, jnp.float32),
            pltpu.VMEM((2, nz) + scale, jnp.float32),
            pltpu.VMEM((2, rest) + scale, jnp.float32),
            dma((nz + 1,)),
            dma((2,)),
            dma((2, nz, 2, 2)),
            dma((2, nz, 2, 2)),
            dma((2, rest, 2, 2)),
        ],
        compiler_params=pltpu.CompilerParams(
            collective_id=0, has_side_effects=True, vmem_limit_bytes=24 * 1024 * 1024
        ),
        cost_estimate=pl.CostEstimate(
            flops=2 * acts.size * rows,
            bytes_accessed=16 * (acts.size + upstream.size),
            transcendentals=0,
        ),
        name="reduce_kept",
    )(keep_lists.T, acts, upstream)


NN = (((1,), (0,)), ((), ()))
NT = (((1,), (1,)), ((), ()))


def split(value):
    high = value.astype(jnp.bfloat16)
    return high, (value - high.astype(jnp.float32)).astype(jnp.bfloat16)


def product3(left, right, dims):
    dot = functools.partial(
        lax.dot_general, dimension_numbers=dims, preferred_element_type=jnp.float32
    )
    (lh, ll), (rh, rl) = left, right
    return dot(lh, rh) + (dot(lh, rl) + dot(ll, rh))


def states_kernel(
    kept, grad_ref, left_gram, right_gram, left_basis, right_basis, moment,
    new_left, new_right, direction,
):
    for slot in range(kept):
        across = grad_ref[slot * BLOCK : (slot + 1) * BLOCK, :]
        down = across.T
        for part in range(LANES // BLOCK):
            at = (0, 0, part * kept + slot)
            span = slice(part * BLOCK, (part + 1) * BLOCK)
            block, turned = split(down[span, :]), split(across[:, span])
            left, right = left_basis[at], right_basis[at]
            left2, right2 = split(left), split(right)
            new_left[at] = 0.95 * left_gram[at] + 0.05 * product3(block, block, NT)
            new_right[at] = 0.95 * right_gram[at] + 0.05 * product3(turned, turned, NT)
            partial_rot = product3(split(left.T), block, NN)
            rotated = product3(split(partial_rot), right2, NN)
            second = 0.95 * moment[at] + 0.05 * rotated * rotated
            scaled = rotated / (jnp.sqrt(second) + 1e-08)
            partial_back = product3(left2, split(scaled), NN)
            direction[at] = product3(split(partial_back), right2, NT)


def update_states(arrived, left_gram, right_gram, left_basis, right_basis, second_moment):
    vmem = pl.BlockSpec(memory_space=pltpu.VMEM)
    return pl.pallas_call(
        functools.partial(states_kernel, arrived.shape[0] // BLOCK),
        out_shape=(jax.ShapeDtypeStruct(left_gram.shape, jnp.float32),) * 3,
        in_specs=[vmem] * 6,
        out_specs=(vmem,) * 3,
        compiler_params=pltpu.CompilerParams(vmem_limit_bytes=16 * 1024 * 1024),
        name="update_states",
    )(arrived, left_gram, right_gram, left_basis, right_basis, second_moment)


def per_device(
    acts, upstream, keep_lists, left_gram, right_gram, left_basis, right_basis, second_moment
):
    share_rows = acts.shape[1]
    share_blocks = share_rows // BLOCK
    kept = keep_lists.shape[1]
    data_size = lax.axis_size("dp")
    fits = (
        lax.axis_size("seq") == 2
        and data_size % 4 == 0
        and share_rows == data_size * LANES
        and kept % 2 == 0
        and upstream.shape[0] % LANES == 0
    )
    if fits:
        arrived = reduced_blocks(acts, upstream, keep_lists, data_size // 4)
        return update_states(
            arrived, left_gram, right_gram, left_basis, right_basis, second_moment
        )
    else:
        kept_share = lax.dynamic_slice_in_dim(
            keep_lists, lax.axis_index("seq") * share_blocks, share_blocks, 0
        )
        gathered = lax.all_gather(upstream, "seq", axis=0, tiled=True)
        grad = lax.dot_general(
            acts, gathered, (((0,), (0,)), ((), ())), preferred_element_type=jnp.float32
        )
        tiles = grad.reshape(share_blocks, BLOCK, grad.shape[1] // BLOCK, BLOCK)
        picked = jnp.take_along_axis(tiles, kept_share[:, None, :, None], axis=2)
        outgoing = picked.transpose(0, 2, 1, 3).reshape(data_size, -1, BLOCK * BLOCK)
        owned_sum = lax.psum_scatter(outgoing, "dp", scatter_dimension=0)
        gradient = owned_sum.reshape(1, 1, -1, BLOCK, BLOCK)
    return precondition(
        gradient, left_gram, right_gram, left_basis, right_basis, second_moment
    )


def solution(mesh):
    block = P("seq", "dp", None, None, None)
    return jax.shard_map(
        per_device,
        mesh=mesh,
        in_specs=(P("dp", "seq"), P(("dp", "seq"), None), P()) + (block,) * 5,
        out_specs=(block,) * 3,
        check_vma=False,
    )
```

```python
import functools

import jax
import jax.numpy as jnp
from jax import lax
from jax.experimental import pallas as pl
from jax.experimental.pallas import tpu as pltpu
from jax.sharding import PartitionSpec as P

BLOCK = 64
LANES = 128
TOP = 32766.0
MESH = pl.DeviceIdType.MESH


def precondition(gradient, left_gram, right_gram, left_basis, right_basis, second_moment):
    highest = lax.Precision.HIGHEST
    new_left = 0.95 * left_gram + 0.05 * jnp.einsum(
        "...ij,...kj->...ik", gradient, gradient, precision=highest
    )
    new_right = 0.95 * right_gram + 0.05 * jnp.einsum(
        "...ji,...jk->...ik", gradient, gradient, precision=highest
    )
    partial_rot = jnp.einsum("...ji,...jk->...ik", left_basis, gradient, precision=highest)
    rotated = jnp.einsum("...ij,...jk->...ik", partial_rot, right_basis, precision=highest)
    second = 0.95 * second_moment + 0.05 * rotated * rotated
    scaled = rotated / (jnp.sqrt(second) + 1e-08)
    partial_back = jnp.einsum("...ij,...jk->...ik", left_basis, scaled, precision=highest)
    direction = jnp.einsum("...ij,...kj->...ik", partial_back, right_basis, precision=highest)
    return (new_left, new_right, direction)


def encode(value):
    peak = jnp.maximum(jnp.max(jnp.abs(value), axis=0, keepdims=True), 1e-30)
    coded = jnp.round(value * (TOP / peak)).astype(jnp.int32).astype(jnp.int16)
    return coded, peak * (1.0 / TOP)


def decode(coded, scale):
    return coded.astype(jnp.int32).astype(jnp.float32) * scale


def split(value):
    high = value.astype(jnp.bfloat16)
    return high, (value - high.astype(jnp.float32)).astype(jnp.bfloat16)


def stacked(left, right):
    out = jnp.dot(left, right, preferred_element_type=jnp.float32)
    rows, columns = out.shape[0] // 2, out.shape[1] // 2
    return out[:rows, :columns] + (out[:rows, columns:] + out[rows:, :columns])


def rows_of(value):
    return jnp.concatenate(split(value), axis=0)


def beside(value):
    return jnp.concatenate(split(value), axis=1)


def diagonal(pair, low):
    return jnp.concatenate([jnp.where(low, pair, 0.0), jnp.where(low, 0.0, pair)], axis=0)


def own_halves(value, low):
    return jnp.where(low, value[:BLOCK], value[BLOCK:])


def prepare(slot, kept, low, states, ready):
    _, _, left_basis, right_basis, moment = states
    left_by, left_turned, right_rows, right_turned, moment_turned = ready
    pair = (slot, kept + slot)
    left = jnp.concatenate([left_basis[at] for at in pair], axis=1)
    left_by[slot] = beside(diagonal(left, low))
    left_t = jnp.concatenate([left_basis[at].T for at in pair], axis=1)
    left_turned[slot] = beside(diagonal(left_t, low))
    right_rows[slot] = rows_of(jnp.concatenate([right_basis[at] for at in pair], axis=0))
    right_turned[slot] = rows_of(jnp.concatenate([right_basis[at].T for at in pair], axis=0))
    moment_turned[slot] = jnp.concatenate([moment[at].T for at in pair], axis=1)


def update(slots, blocks, kept, low, states, ready, outs):
    left_gram, right_gram = states[:2]
    left_by, left_turned, right_rows, right_turned, moment_turned = ready
    new_left, new_right, direction = outs
    parts = (slice(0, BLOCK), slice(BLOCK, LANES))
    partial = [stacked(rows_of(t), left_by[k]) for k, t in zip(slots, blocks)]
    turned = [t.T for t in blocks]
    rotated = [
        own_halves(stacked(right_turned[k], beside(p)), low) for k, p in zip(slots, partial)
    ]
    scaled = [
        r / (jnp.sqrt(0.95 * moment_turned[k] + 0.05 * r * r) + 1e-08)
        for k, r in zip(slots, rotated)
    ]
    back = [stacked(rows_of(v), left_turned[k]) for k, v in zip(slots, scaled)]
    for k, t, u in zip(slots, blocks, turned):
        outer = stacked(rows_of(u), beside(t))
        masked = split(jnp.concatenate([jnp.where(low, t, 0.0), jnp.where(low, 0.0, t)], axis=0))
        halves = split(u)
        dot = functools.partial(jnp.dot, preferred_element_type=jnp.float32)
        inner = dot(masked[0], halves[0]) + (
            dot(masked[0], halves[1]) + dot(masked[1], halves[0])
        )
        for part, span in enumerate(parts):
            at = part * kept + k
            new_left[0, 0, at] = 0.95 * left_gram[at] + 0.05 * outer[span, span]
            new_right[0, 0, at] = 0.95 * right_gram[at] + 0.05 * inner[span]
    for k, q in zip(slots, back):
        result = own_halves(stacked(right_rows[k], beside(q)), low).T
        for part, span in enumerate(parts):
            direction[0, 0, part * kept + k] = result[span]


def reduce_kernel(
    nz, kept, keep_ref, acts_hbm, up_hbm,
    left_gram, right_gram, left_basis, right_basis, moment,
    new_left, new_right, direction,
    acts, up, upt, product, acc, states,
    left_by, left_turned, right_rows, right_turned, moment_turned,
    send1, send2, send3, recv1, recv2, recv3,
    ssend1, ssend2, ssend3, srecv1, srecv2, srecv3,
    load_sems, state_sems, up_sems, sems1, sems2, sems3,
):
    dp, seq = lax.axis_index("dp"), lax.axis_index("seq")
    x, y, z = lax.rem(dp, 2), lax.rem(dp // 2, 2), dp // 4
    ox, oy = 1 - x, 1 - y
    x_peer = (z * 2 + y) * 2 + ox
    y_peer = (z * 2 + oy) * 2 + x
    first_peer = (x_peer, y_peer)
    second_peer = (y_peer, x_peer)

    def z_target(step):
        last = step // max(nz - 1, 1)
        return lax.rem(z + (1 - last) * (lax.rem(step + nz // 2 - 1, max(nz - 1, 1)) + 1), nz)

    def z_peer(step):
        return (z_target(step) * 2 + y) * 2 + x

    width = 4 * LANES

    def load(step):
        columns = pl.ds(pl.multiple_of(z_target(step) * width, width), width)
        return pltpu.make_async_copy(
            acts_hbm.at[:, columns], acts.at[step], load_sems.at[step + 1]
        )

    up_load = pltpu.make_async_copy(up_hbm, up, load_sems.at[0])
    up_load.start()
    for step in range(nz):
        load(step).start()

    state_loads = [
        pltpu.make_async_copy(ref.at[0, 0], states.at[i], state_sems.at[i])
        for i, ref in enumerate((left_gram, right_gram, left_basis, right_basis, moment))
    ]
    for state_load in state_loads:
        state_load.start()
    held = tuple(states.at[i] for i in range(len(state_loads)))
    ready = (left_by, left_turned, right_rows, right_turned, moment_turned)

    barrier = pltpu.get_barrier_semaphore()
    pl.semaphore_signal(barrier, inc=1, device_id=(dp, 1 - seq), device_id_type=MESH)
    for peer in (x_peer, y_peer) + tuple(z_peer(step) for step in range(nz - 1)):
        pl.semaphore_signal(barrier, inc=1, device_id=(peer, seq), device_id_type=MESH)
    up_load.wait()
    upt[seq] = up[...].T
    pl.semaphore_wait(barrier, nz + 2)

    def remote(src, dst, sems, peer):
        return pltpu.make_async_remote_copy(
            src_ref=src, dst_ref=dst, send_sem=sems.at[0], recv_sem=sems.at[1],
            device_id=peer, device_id_type=MESH,
        )

    up_copy = remote(upt.at[seq], upt.at[seq], up_sems, (dp, 1 - seq))
    up_copy.start()
    up_copy.wait()

    half_slots = kept // 2
    blocks = 8 * nz
    low = lax.broadcasted_iota(jnp.int32, (BLOCK, LANES), 1) < BLOCK

    def copies1(half, step):
        peer = (first_peer[half], seq)
        return (
            remote(send1.at[half, step], recv1.at[half, step], sems1.at[half, step, 0], peer),
            remote(ssend1.at[half, step], srecv1.at[half, step], sems1.at[half, step, 1], peer),
        )

    def copies2(half, step):
        peer = (second_peer[half], seq)
        return (
            remote(send2.at[half, step], recv2.at[half, step], sems2.at[half, step, 0], peer),
            remote(ssend2.at[half, step], srecv2.at[half, step], sems2.at[half, step, 1], peer),
        )

    def copies3(half, step):
        peer = (z_peer(step), seq)
        return (
            remote(send3.at[half, step], recv3.at[half, step], sems3.at[half, step, 0], peer),
            remote(ssend3.at[half, step], srecv3.at[half, step], sems3.at[half, step, 1], peer),
        )

    def produce(step):
        load(step).wait()
        for dy in (1, 0):
            to_y = y if dy == 0 else oy
            columns = pl.ds(pl.multiple_of(to_y * (2 * LANES), 2 * LANES), 2 * LANES)
            whole = jnp.dot(
                jnp.concatenate([upt[0], upt[1]], axis=1),
                acts[step, :, columns],
                preferred_element_type=jnp.float32,
            )
            product[0] = whole[:, :LANES].reshape(-1, BLOCK, LANES)
            product[1] = whole[:, LANES:].reshape(-1, BLOCK, LANES)
            for dx in (1, 0):
                to_x = x if dx == 0 else ox
                row_block = seq * blocks + ((z_target(step) * 2 + to_y) * 2 + to_x) * 2
                for half in range(2):
                    parts = []
                    for slot in range(half * half_slots, (half + 1) * half_slots):
                        top = keep_ref[slot, row_block]
                        bottom = keep_ref[slot, row_block + 1]
                        parts.append(
                            jnp.where(low, product[to_x, top], product[to_x, bottom])
                        )
                    value = jnp.concatenate(parts, axis=0)
                    away, slot = ((dx, dy), (dy, dx))[half]
                    if away:
                        coded, scale = encode(value)
                        send1[half, step, slot] = coded
                        ssend1[half, step, slot] = jnp.broadcast_to(scale, (8, LANES))
                    else:
                        acc[half, step, slot] = value
            for copy in copies1(dy, step):
                copy.start()

    def forward(step):
        for half in (1, 0):
            for copy in copies1(half, step):
                copy.wait_recv()
            away = acc[half, step, 1] + decode(
                recv1[half, step, 1], srecv1[half, step, 1, 0:1, :]
            )
            coded, scale = encode(away)
            send2[half, step] = coded
            ssend2[half, step] = jnp.broadcast_to(scale, (8, LANES))
            for copy in copies2(half, step):
                copy.start()
            acc[half, step, 0] += decode(recv1[half, step, 0], srecv1[half, step, 0, 0:1, :])

    def settle(step, half):
        for copy in copies2(half, step):
            copy.wait_recv()
        return acc[half, step, 0] + decode(recv2[half, step], srecv2[half, step, 0:1, :])

    def spread(step):
        for half in (1, 0):
            coded, scale = encode(settle(step, half))
            send3[half, step] = coded
            ssend3[half, step] = jnp.broadcast_to(scale, (8, LANES))
            for copy in copies3(half, step):
                copy.start()

    def turn(step, carry):
        @pl.when(step < nz)
        def _():
            produce(step)

        @pl.when(step == 1)
        def _():
            for state_load in state_loads:
                state_load.wait()
            for slot in range(kept):
                prepare(slot, kept, low, held, ready)

        @pl.when(step >= 1)
        def _():
            forward(step - 1)

        @pl.when(step >= 2)
        def _():
            spread(step - 2)

        return carry

    lax.fori_loop(0, nz + 1, turn, 0)

    for half in (1, 0):
        total = settle(nz - 1, half)
        for step in range(nz - 1):
            for copy in copies3(half, step):
                copy.wait_recv()
            total += decode(recv3[half, step], srecv3[half, step, 0:1, :])
        update(
            tuple(range(half * half_slots, (half + 1) * half_slots)),
            [total[i * BLOCK : (i + 1) * BLOCK] for i in range(half_slots)],
            kept, low, held, ready, (new_left, new_right, direction),
        )

    for half in range(2):
        for step in range(nz):
            for copy in copies1(half, step) + copies2(half, step):
                copy.wait_send()
            if step < nz - 1:
                for copy in copies3(half, step):
                    copy.wait_send()


def fused_step(acts, upstream, keep_lists, states, nz):
    kept = keep_lists.shape[1]
    half_rows = kept // 2 * BLOCK
    tokens, rows = upstream.shape[0], upstream.shape[1]
    rest = max(nz - 1, 1)
    half = (half_rows, LANES)
    scale = (8, LANES)
    dma = pltpu.SemaphoreType.DMA
    vmem, hbm = (pl.BlockSpec(memory_space=space) for space in (pltpu.VMEM, pltpu.HBM))
    return pl.pallas_call(
        functools.partial(reduce_kernel, nz, kept),
        out_shape=(jax.ShapeDtypeStruct(states[0].shape, jnp.float32),) * 3,
        in_specs=[pl.BlockSpec(memory_space=pltpu.SMEM)] + [hbm] * (2 + len(states)),
        out_specs=(vmem,) * 3,
        scratch_shapes=[
            pltpu.VMEM((nz, acts.shape[0], 4 * LANES), jnp.bfloat16),
            pltpu.VMEM(upstream.shape, jnp.bfloat16),
            pltpu.VMEM((2, rows, tokens), jnp.bfloat16),
            pltpu.VMEM((2, rows // BLOCK, BLOCK, LANES), jnp.float32),
            pltpu.VMEM((2, nz, 2) + half, jnp.float32),
            pltpu.VMEM((len(states),) + states[0].shape[2:], jnp.float32),
            pltpu.VMEM((kept, LANES, 2 * LANES), jnp.bfloat16),
            pltpu.VMEM((kept, LANES, 2 * LANES), jnp.bfloat16),
            pltpu.VMEM((kept, 2 * LANES, BLOCK), jnp.bfloat16),
            pltpu.VMEM((kept, 2 * LANES, BLOCK), jnp.bfloat16),
            pltpu.VMEM((kept, BLOCK, LANES), jnp.float32),
            pltpu.VMEM((2, nz, 2) + half, jnp.int16),
            pltpu.VMEM((2, nz) + half, jnp.int16),
            pltpu.VMEM((2, rest) + half, jnp.int16),
            pltpu.VMEM((2, nz, 2) + half, jnp.int16),
            pltpu.VMEM((2, nz) + half, jnp.int16),
            pltpu.VMEM((2, rest) + half, jnp.int16),
            pltpu.VMEM((2, nz, 2) + scale, jnp.float32),
            pltpu.VMEM((2, nz) + scale, jnp.float32),
            pltpu.VMEM((2, rest) + scale, jnp.float32),
            pltpu.VMEM((2, nz, 2) + scale, jnp.float32),
            pltpu.VMEM((2, nz) + scale, jnp.float32),
            pltpu.VMEM((2, rest) + scale, jnp.float32),
            dma((nz + 1,)),
            dma((len(states),)),
            dma((2,)),
            dma((2, nz, 2, 2)),
            dma((2, nz, 2, 2)),
            dma((2, rest, 2, 2)),
        ],
        compiler_params=pltpu.CompilerParams(
            collective_id=0, has_side_effects=True, vmem_limit_bytes=60 * 1024 * 1024
        ),
        cost_estimate=pl.CostEstimate(
            flops=2 * acts.size * rows,
            bytes_accessed=16 * (acts.size + upstream.size),
            transcendentals=0,
        ),
        name="fused_step",
    )(keep_lists.T, acts, upstream, *states)


def per_device(
    acts, upstream, keep_lists, left_gram, right_gram, left_basis, right_basis, second_moment
):
    share_rows = acts.shape[1]
    share_blocks = share_rows // BLOCK
    kept = keep_lists.shape[1]
    data_size = lax.axis_size("dp")
    fits = (
        lax.axis_size("seq") == 2
        and data_size % 4 == 0
        and share_rows == data_size * LANES
        and kept % 2 == 0
        and upstream.shape[0] % LANES == 0
    )
    if fits:
        states = (left_gram, right_gram, left_basis, right_basis, second_moment)
        return fused_step(acts, upstream, keep_lists, states, data_size // 4)
    else:
        kept_share = lax.dynamic_slice_in_dim(
            keep_lists, lax.axis_index("seq") * share_blocks, share_blocks, 0
        )
        gathered = lax.all_gather(upstream, "seq", axis=0, tiled=True)
        grad = lax.dot_general(
            acts, gathered, (((0,), (0,)), ((), ())), preferred_element_type=jnp.float32
        )
        tiles = grad.reshape(share_blocks, BLOCK, grad.shape[1] // BLOCK, BLOCK)
        picked = jnp.take_along_axis(tiles, kept_share[:, None, :, None], axis=2)
        outgoing = picked.transpose(0, 2, 1, 3).reshape(data_size, -1, BLOCK * BLOCK)
        owned_sum = lax.psum_scatter(outgoing, "dp", scatter_dimension=0)
        gradient = owned_sum.reshape(1, 1, -1, BLOCK, BLOCK)
    return precondition(
        gradient, left_gram, right_gram, left_basis, right_basis, second_moment
    )


def solution(mesh):
    block = P("seq", "dp", None, None, None)
    return jax.shard_map(
        per_device,
        mesh=mesh,
        in_specs=(P("dp", "seq"), P(("dp", "seq"), None), P()) + (block,) * 5,
        out_specs=(block,) * 3,
        check_vma=False,
    )
```

```python
import functools

import jax
import jax.numpy as jnp
from jax import lax
from jax.experimental import pallas as pl
from jax.experimental.pallas import tpu as pltpu
from jax.sharding import PartitionSpec as P

BLOCK = 64
LANES = 128
TOP = 32766.0
GRANT = 65000 * 1024
MESH = pl.DeviceIdType.MESH


def precondition(gradient, left_gram, right_gram, left_basis, right_basis, second_moment):
    highest = lax.Precision.HIGHEST
    new_left = 0.95 * left_gram + 0.05 * jnp.einsum(
        "...ij,...kj->...ik", gradient, gradient, precision=highest
    )
    new_right = 0.95 * right_gram + 0.05 * jnp.einsum(
        "...ji,...jk->...ik", gradient, gradient, precision=highest
    )
    partial_rot = jnp.einsum("...ji,...jk->...ik", left_basis, gradient, precision=highest)
    rotated = jnp.einsum("...ij,...jk->...ik", partial_rot, right_basis, precision=highest)
    second = 0.95 * second_moment + 0.05 * rotated * rotated
    scaled = rotated / (jnp.sqrt(second) + 1e-08)
    partial_back = jnp.einsum("...ij,...jk->...ik", left_basis, scaled, precision=highest)
    direction = jnp.einsum("...ij,...kj->...ik", partial_back, right_basis, precision=highest)
    return (new_left, new_right, direction)


def encode(value):
    peak = jnp.maximum(jnp.max(jnp.abs(value), axis=0, keepdims=True), 1e-30)
    coded = jnp.round(value * (TOP / peak)).astype(jnp.int32).astype(jnp.int16)
    return coded, peak * (1.0 / TOP)


def decode(coded, scale):
    return coded.astype(jnp.int32).astype(jnp.float32) * scale


def split(value):
    high = value.astype(jnp.bfloat16)
    return high, (value - high.astype(jnp.float32)).astype(jnp.bfloat16)


def stacked(left, right):
    out = jnp.dot(left, right, preferred_element_type=jnp.float32)
    rows, columns = out.shape[0] // 2, out.shape[1] // 2
    return out[:rows, :columns] + (out[:rows, columns:] + out[rows:, :columns])


def rows_of(value):
    return jnp.concatenate(split(value), axis=0)


def beside(value):
    return jnp.concatenate(split(value), axis=1)


def diagonal(pair, low):
    return jnp.concatenate([jnp.where(low, pair, 0.0), jnp.where(low, 0.0, pair)], axis=0)


def own_halves(value, low):
    return jnp.where(low, value[:BLOCK], value[BLOCK:])


def prepare(slot, kept, low, states, ready):
    _, _, left_basis, right_basis, moment = states
    left_by, left_turned, right_rows, right_turned, moment_turned = ready
    pair = (slot, kept + slot)
    left = jnp.concatenate([left_basis[at] for at in pair], axis=1)
    left_by[slot] = beside(diagonal(left, low))
    left_t = jnp.concatenate([left_basis[at].T for at in pair], axis=1)
    left_turned[slot] = beside(diagonal(left_t, low))
    right_rows[slot] = rows_of(jnp.concatenate([right_basis[at] for at in pair], axis=0))
    right_turned[slot] = rows_of(jnp.concatenate([right_basis[at].T for at in pair], axis=0))
    moment_turned[slot] = jnp.concatenate([moment[at].T for at in pair], axis=1)


def update(slots, blocks, kept, low, states, ready, outs):
    left_gram, right_gram = states[:2]
    left_by, left_turned, right_rows, right_turned, moment_turned = ready
    new_left, new_right, direction = outs
    parts = (slice(0, BLOCK), slice(BLOCK, LANES))
    partial = [stacked(rows_of(t), left_by[k]) for k, t in zip(slots, blocks)]
    turned = [t.T for t in blocks]
    rotated = [
        own_halves(stacked(right_turned[k], beside(p)), low) for k, p in zip(slots, partial)
    ]
    scaled = [
        r / (jnp.sqrt(0.95 * moment_turned[k] + 0.05 * r * r) + 1e-08)
        for k, r in zip(slots, rotated)
    ]
    back = [stacked(rows_of(v), left_turned[k]) for k, v in zip(slots, scaled)]
    for k, t, u in zip(slots, blocks, turned):
        outer = stacked(rows_of(u), beside(t))
        masked = split(jnp.concatenate([jnp.where(low, t, 0.0), jnp.where(low, 0.0, t)], axis=0))
        halves = split(u)
        dot = functools.partial(jnp.dot, preferred_element_type=jnp.float32)
        inner = dot(masked[0], halves[0]) + (
            dot(masked[0], halves[1]) + dot(masked[1], halves[0])
        )
        for part, span in enumerate(parts):
            at = part * kept + k
            new_left[0, 0, at] = 0.95 * left_gram[at] + 0.05 * outer[span, span]
            new_right[0, 0, at] = 0.95 * right_gram[at] + 0.05 * inner[span]
    for k, q in zip(slots, back):
        result = own_halves(stacked(right_rows[k], beside(q)), low).T
        for part, span in enumerate(parts):
            direction[0, 0, part * kept + k] = result[span]


def reduce_kernel(
    nz, kept, keep_ref, acts_hbm, up_hbm,
    left_gram, right_gram, left_basis, right_basis, moment,
    new_left, new_right, direction,
    acts, up, upt, product, acc, states,
    left_by, left_turned, right_rows, right_turned, moment_turned,
    send1, send2, send3, recv1, recv2, recv3,
    ssend1, ssend2, ssend3, srecv1, srecv2, srecv3,
    load_sems, state_sems, up_sems, sems1, sems2, sems3,
):
    dp, seq = lax.axis_index("dp"), lax.axis_index("seq")
    x, y, z = lax.rem(dp, 2), lax.rem(dp // 2, 2), dp // 4
    ox, oy = 1 - x, 1 - y
    x_peer = (z * 2 + y) * 2 + ox
    y_peer = (z * 2 + oy) * 2 + x
    first_peer = (x_peer, y_peer)
    second_peer = (y_peer, x_peer)

    def z_target(step):
        turn_z = step // 2
        last = turn_z // max(nz - 1, 1)
        return lax.rem(z + (1 - last) * (lax.rem(turn_z + nz // 2 - 1, max(nz - 1, 1)) + 1), nz)

    def z_peer(step):
        return (z_target(step) * 2 + y) * 2 + x

    width = 4 * LANES

    def load(turn_z):
        columns = pl.ds(pl.multiple_of(z_target(2 * turn_z) * width, width), width)
        return pltpu.make_async_copy(
            acts_hbm.at[:, columns], acts.at[turn_z], load_sems.at[turn_z + 1]
        )

    up_load = pltpu.make_async_copy(up_hbm, up, load_sems.at[0])
    up_load.start()
    for turn_z in range(nz):
        load(turn_z).start()

    state_loads = [
        pltpu.make_async_copy(ref.at[0, 0], states.at[i], state_sems.at[i])
        for i, ref in enumerate((left_gram, right_gram, left_basis, right_basis, moment))
    ]
    for state_load in state_loads:
        state_load.start()
    held = tuple(states.at[i] for i in range(len(state_loads)))
    ready = (left_by, left_turned, right_rows, right_turned, moment_turned)

    barrier = pltpu.get_barrier_semaphore()
    pl.semaphore_signal(barrier, inc=1, device_id=(dp, 1 - seq), device_id_type=MESH)
    for peer in (x_peer, y_peer) + tuple(z_peer(2 * turn_z) for turn_z in range(nz - 1)):
        pl.semaphore_signal(barrier, inc=1, device_id=(peer, seq), device_id_type=MESH)
    up_load.wait()
    upt[seq] = up[...].T
    pl.semaphore_wait(barrier, nz + 2)

    def remote(src, dst, sems, peer):
        return pltpu.make_async_remote_copy(
            src_ref=src, dst_ref=dst, send_sem=sems.at[0], recv_sem=sems.at[1],
            device_id=peer, device_id_type=MESH,
        )

    up_copy = remote(upt.at[seq], upt.at[seq], up_sems, (dp, 1 - seq))
    up_copy.start()
    up_copy.wait()

    half_slots = kept // 2
    run = half_slots // 2
    steps = 2 * nz
    blocks = 8 * nz
    low = lax.broadcasted_iota(jnp.int32, (BLOCK, LANES), 1) < BLOCK

    def copies1(half, step):
        peer = (first_peer[half], seq)
        return (
            remote(send1.at[half, step], recv1.at[half, step], sems1.at[half, step, 0], peer),
            remote(ssend1.at[half, step], srecv1.at[half, step], sems1.at[half, step, 1], peer),
        )

    def copies2(half, step):
        peer = (second_peer[half], seq)
        return (
            remote(send2.at[half, step], recv2.at[half, step], sems2.at[half, step, 0], peer),
            remote(ssend2.at[half, step], srecv2.at[half, step], sems2.at[half, step, 1], peer),
        )

    def copies3(half, step):
        peer = (z_peer(step), seq)
        return (
            remote(send3.at[half, step], recv3.at[half, step], sems3.at[half, step, 0], peer),
            remote(ssend3.at[half, step], srecv3.at[half, step], sems3.at[half, step, 1], peer),
        )

    def multiply(turn_z):
        load(turn_z).wait()
        for dy in (1, 0):
            to_y = y if dy == 0 else oy
            columns = pl.ds(pl.multiple_of(to_y * (2 * LANES), 2 * LANES), 2 * LANES)
            whole = jnp.dot(
                jnp.concatenate([upt[0], upt[1]], axis=1),
                acts[turn_z, :, columns],
                preferred_element_type=jnp.float32,
            )
            product[dy, 0] = whole[:, :LANES].reshape(-1, BLOCK, LANES)
            product[dy, 1] = whole[:, LANES:].reshape(-1, BLOCK, LANES)

    def produce(step):
        for dy in (1, 0):
            to_y = y if dy == 0 else oy
            for dx in (1, 0):
                to_x = x if dx == 0 else ox
                row_block = seq * blocks + ((z_target(step) * 2 + to_y) * 2 + to_x) * 2
                for half in range(2):
                    parts = []
                    for i in range(run):
                        slot = half * half_slots + lax.rem(step, 2) * run + i
                        top = keep_ref[slot, row_block]
                        bottom = keep_ref[slot, row_block + 1]
                        parts.append(
                            jnp.where(low, product[dy, to_x, top], product[dy, to_x, bottom])
                        )
                    value = jnp.concatenate(parts, axis=0)
                    away, place = ((dx, dy), (dy, dx))[half]
                    if away:
                        coded, scale = encode(value)
                        send1[half, step, place] = coded
                        ssend1[half, step, place] = jnp.broadcast_to(scale, (8, LANES))
                    else:
                        acc[half, step, place] = value
            for copy in copies1(dy, step):
                copy.start()

    def forward(step):
        for half in (1, 0):
            for copy in copies1(half, step):
                copy.wait_recv()
            away = acc[half, step, 1] + decode(
                recv1[half, step, 1], srecv1[half, step, 1, 0:1, :]
            )
            coded, scale = encode(away)
            send2[half, step] = coded
            ssend2[half, step] = jnp.broadcast_to(scale, (8, LANES))
            for copy in copies2(half, step):
                copy.start()
            acc[half, step, 0] += decode(recv1[half, step, 0], srecv1[half, step, 0, 0:1, :])

    def settle(step, half):
        for copy in copies2(half, step):
            copy.wait_recv()
        return acc[half, step, 0] + decode(recv2[half, step], srecv2[half, step, 0:1, :])

    def spread(step):
        for half in (1, 0):
            coded, scale = encode(settle(step, half))
            send3[half, step] = coded
            ssend3[half, step] = jnp.broadcast_to(scale, (8, LANES))
            for copy in copies3(half, step):
                copy.start()

    def turn(step, carry):
        @pl.when((step < steps) & (lax.rem(step, 2) == 0))
        def _():
            multiply(step // 2)

        @pl.when(step < steps)
        def _():
            produce(step)

        @pl.when(step == 1)
        def _():
            for state_load in state_loads:
                state_load.wait()

        @pl.when(step >= 1)
        def _():
            for i in range(kept // steps):
                prepare((step - 1) * (kept // steps) + i, kept, low, held, ready)
            forward(step - 1)

        @pl.when((step >= 2) & (step < steps))
        def _():
            spread(step - 2)

        return carry

    lax.fori_loop(0, steps + 1, turn, 0)

    for odd in range(2):
        slots, blocks_done = [], []
        for half in (1, 0):
            total = settle(steps - 2 + odd, half)
            for step in range(odd, steps - 2, 2):
                for copy in copies3(half, step):
                    copy.wait_recv()
                total += decode(recv3[half, step], srecv3[half, step, 0:1, :])
            for i in range(run):
                slots.append(half * half_slots + odd * run + i)
                blocks_done.append(total[i * BLOCK : (i + 1) * BLOCK])
        update(
            slots, blocks_done, kept, low, held, ready, (new_left, new_right, direction)
        )

    for half in range(2):
        for step in range(steps):
            for copy in copies1(half, step) + copies2(half, step):
                copy.wait_send()
            if step < steps - 2:
                for copy in copies3(half, step):
                    copy.wait_send()


def fused_step(acts, upstream, keep_lists, states, nz):
    kept = keep_lists.shape[1]
    tokens, rows = upstream.shape[0], upstream.shape[1]
    steps = 2 * nz
    rest = max(steps - 2, 1)
    half = (kept // 4 * BLOCK, LANES)
    scale = (8, LANES)
    dma = pltpu.SemaphoreType.DMA
    vmem, hbm = (pl.BlockSpec(memory_space=space) for space in (pltpu.VMEM, pltpu.HBM))
    return pl.pallas_call(
        functools.partial(reduce_kernel, nz, kept),
        out_shape=(jax.ShapeDtypeStruct(states[0].shape, jnp.float32),) * 3,
        in_specs=[pl.BlockSpec(memory_space=pltpu.SMEM)] + [hbm] * (2 + len(states)),
        out_specs=(vmem,) * 3,
        scratch_shapes=[
            pltpu.VMEM((nz, acts.shape[0], 4 * LANES), jnp.bfloat16),
            pltpu.VMEM(upstream.shape, jnp.bfloat16),
            pltpu.VMEM((2, rows, tokens), jnp.bfloat16),
            pltpu.VMEM((2, 2, rows // BLOCK, BLOCK, LANES), jnp.float32),
            pltpu.VMEM((2, steps, 2) + half, jnp.float32),
            pltpu.VMEM((len(states),) + states[0].shape[2:], jnp.float32),
            pltpu.VMEM((kept, LANES, 2 * LANES), jnp.bfloat16),
            pltpu.VMEM((kept, LANES, 2 * LANES), jnp.bfloat16),
            pltpu.VMEM((kept, 2 * LANES, BLOCK), jnp.bfloat16),
            pltpu.VMEM((kept, 2 * LANES, BLOCK), jnp.bfloat16),
            pltpu.VMEM((kept, BLOCK, LANES), jnp.float32),
            pltpu.VMEM((2, steps, 2) + half, jnp.int16),
            pltpu.VMEM((2, steps) + half, jnp.int16),
            pltpu.VMEM((2, rest) + half, jnp.int16),
            pltpu.VMEM((2, steps, 2) + half, jnp.int16),
            pltpu.VMEM((2, steps) + half, jnp.int16),
            pltpu.VMEM((2, rest) + half, jnp.int16),
            pltpu.VMEM((2, steps, 2) + scale, jnp.float32),
            pltpu.VMEM((2, steps) + scale, jnp.float32),
            pltpu.VMEM((2, rest) + scale, jnp.float32),
            pltpu.VMEM((2, steps, 2) + scale, jnp.float32),
            pltpu.VMEM((2, steps) + scale, jnp.float32),
            pltpu.VMEM((2, rest) + scale, jnp.float32),
            dma((nz + 1,)),
            dma((len(states),)),
            dma((2,)),
            dma((2, steps, 2, 2)),
            dma((2, steps, 2, 2)),
            dma((2, rest, 2, 2)),
        ],
        compiler_params=pltpu.CompilerParams(
            collective_id=0, has_side_effects=True, vmem_limit_bytes=GRANT
        ),
        cost_estimate=pl.CostEstimate(
            flops=2 * acts.size * rows,
            bytes_accessed=16 * (acts.size + upstream.size),
            transcendentals=0,
        ),
        name="fused_step",
    )(keep_lists.T, acts, upstream, *states)


def move_kernel(*refs):
    count = len(refs) // 2
    sems = refs[-1]
    copies = [
        pltpu.make_async_copy(refs[i], refs[count + i], sems.at[i]) for i in range(count)
    ]
    for copy in copies:
        copy.start()
    for copy in copies:
        copy.wait()


def moved(arrays):
    anywhere = pl.BlockSpec(memory_space=pl.ANY)
    return pl.pallas_call(
        move_kernel,
        out_shape=tuple(jax.ShapeDtypeStruct(a.shape, a.dtype) for a in arrays),
        in_specs=[anywhere] * len(arrays),
        out_specs=(anywhere,) * len(arrays),
        scratch_shapes=[pltpu.SemaphoreType.DMA((len(arrays),))],
        compiler_params=pltpu.CompilerParams(vmem_limit_bytes=GRANT),
        name="move_out",
    )(*arrays)


def per_device(
    acts, upstream, keep_lists, left_gram, right_gram, left_basis, right_basis, second_moment
):
    share_rows = acts.shape[1]
    share_blocks = share_rows // BLOCK
    kept = keep_lists.shape[1]
    data_size = lax.axis_size("dp")
    fits = (
        lax.axis_size("seq") == 2
        and data_size % 4 == 0
        and share_rows == data_size * LANES
        and kept % (data_size // 2) == 0
        and kept % 4 == 0
        and upstream.shape[0] % LANES == 0
    )
    if fits:
        states = (left_gram, right_gram, left_basis, right_basis, second_moment)
        return moved(fused_step(acts, upstream, keep_lists, states, data_size // 4))
    else:
        kept_share = lax.dynamic_slice_in_dim(
            keep_lists, lax.axis_index("seq") * share_blocks, share_blocks, 0
        )
        gathered = lax.all_gather(upstream, "seq", axis=0, tiled=True)
        grad = lax.dot_general(
            acts, gathered, (((0,), (0,)), ((), ())), preferred_element_type=jnp.float32
        )
        tiles = grad.reshape(share_blocks, BLOCK, grad.shape[1] // BLOCK, BLOCK)
        picked = jnp.take_along_axis(tiles, kept_share[:, None, :, None], axis=2)
        outgoing = picked.transpose(0, 2, 1, 3).reshape(data_size, -1, BLOCK * BLOCK)
        owned_sum = lax.psum_scatter(outgoing, "dp", scatter_dimension=0)
        gradient = owned_sum.reshape(1, 1, -1, BLOCK, BLOCK)
    return precondition(
        gradient, left_gram, right_gram, left_basis, right_basis, second_moment
    )


def solution(mesh):
    block = P("seq", "dp", None, None, None)
    return jax.shard_map(
        per_device,
        mesh=mesh,
        in_specs=(P("dp", "seq"), P(("dp", "seq"), None), P()) + (block,) * 5,
        out_specs=(block,) * 3,
        check_vma=False,
    )
```

```python
import functools

import jax
import jax.numpy as jnp
from jax import lax
from jax.experimental import pallas as pl
from jax.experimental.pallas import tpu as pltpu
from jax.sharding import PartitionSpec as P

BLOCK = 64
LANES = 128
TOP = 32766.0
GRANT = 65000 * 1024
LAG = 2
MESH = pl.DeviceIdType.MESH


def precondition(gradient, left_gram, right_gram, left_basis, right_basis, second_moment):
    highest = lax.Precision.HIGHEST
    new_left = 0.95 * left_gram + 0.05 * jnp.einsum(
        "...ij,...kj->...ik", gradient, gradient, precision=highest
    )
    new_right = 0.95 * right_gram + 0.05 * jnp.einsum(
        "...ji,...jk->...ik", gradient, gradient, precision=highest
    )
    partial_rot = jnp.einsum("...ji,...jk->...ik", left_basis, gradient, precision=highest)
    rotated = jnp.einsum("...ij,...jk->...ik", partial_rot, right_basis, precision=highest)
    second = 0.95 * second_moment + 0.05 * rotated * rotated
    scaled = rotated / (jnp.sqrt(second) + 1e-08)
    partial_back = jnp.einsum("...ij,...jk->...ik", left_basis, scaled, precision=highest)
    direction = jnp.einsum("...ij,...kj->...ik", partial_back, right_basis, precision=highest)
    return (new_left, new_right, direction)


def encode(value):
    peak = jnp.maximum(jnp.max(jnp.abs(value), axis=0, keepdims=True), 1e-30)
    coded = jnp.round(value * (TOP / peak)).astype(jnp.int32).astype(jnp.int16)
    return coded, peak * (1.0 / TOP)


def decode(coded, scale):
    return coded.astype(jnp.int32).astype(jnp.float32) * scale


def split(value):
    high = value.astype(jnp.bfloat16)
    return high, (value - high.astype(jnp.float32)).astype(jnp.bfloat16)


def stacked(left, right):
    out = jnp.dot(left, right, preferred_element_type=jnp.float32)
    rows, columns = out.shape[0] // 2, out.shape[1] // 2
    return out[:rows, :columns] + (out[:rows, columns:] + out[rows:, :columns])


def rows_of(value):
    return jnp.concatenate(split(value), axis=0)


def beside(value):
    return jnp.concatenate(split(value), axis=1)


def diagonal(pair, low):
    return jnp.concatenate([jnp.where(low, pair, 0.0), jnp.where(low, 0.0, pair)], axis=0)


def own_halves(value, low):
    return jnp.where(low, value[:BLOCK], value[BLOCK:])


def prepare(slot, kept, low, states, ready):
    left_gram, right_gram, left_basis, right_basis, moment = states
    left_by, left_turned, right_rows, right_turned, moment_turned, left_pair, right_pair = ready
    pair = (slot, kept + slot)
    left = jnp.concatenate([left_basis[at] for at in pair], axis=1)
    left_by[slot] = beside(diagonal(left, low))
    left_t = jnp.concatenate([left_basis[at].T for at in pair], axis=1)
    left_turned[slot] = beside(diagonal(left_t, low))
    right_rows[slot] = rows_of(jnp.concatenate([right_basis[at] for at in pair], axis=0))
    right_turned[slot] = rows_of(jnp.concatenate([right_basis[at].T for at in pair], axis=0))
    moment_turned[slot] = jnp.concatenate([moment[at].T for at in pair], axis=1)
    left_pair[slot] = jnp.concatenate([left_gram[at] for at in pair], axis=1)
    right_pair[slot] = jnp.concatenate([right_gram[at] for at in pair], axis=1)


def update(slots, blocks, low, ready, outs):
    left_by, left_turned, right_rows, right_turned, moment_turned, left_pair, right_pair = ready
    new_left, new_right, direction = outs
    parts = (slice(0, BLOCK), slice(BLOCK, LANES))
    partial = [stacked(rows_of(t), left_by[k]) for k, t in zip(slots, blocks)]
    turned = [t.T for t in blocks]
    rotated = [
        own_halves(stacked(right_turned[k], beside(p)), low) for k, p in zip(slots, partial)
    ]
    scaled = [
        r / (jnp.sqrt(0.95 * moment_turned[k] + 0.05 * r * r) + 1e-08)
        for k, r in zip(slots, rotated)
    ]
    back = [stacked(rows_of(v), left_turned[k]) for k, v in zip(slots, scaled)]
    for k, t, u in zip(slots, blocks, turned):
        outer = stacked(rows_of(u), beside(t))
        masked = split(jnp.concatenate([jnp.where(low, t, 0.0), jnp.where(low, 0.0, t)], axis=0))
        halves = split(u)
        dot = functools.partial(jnp.dot, preferred_element_type=jnp.float32)
        inner = dot(masked[0], halves[0]) + (
            dot(masked[0], halves[1]) + dot(masked[1], halves[0])
        )
        down = slice(k * BLOCK, (k + 1) * BLOCK)
        new_left[down, :] = 0.95 * left_pair[k] + 0.05 * own_halves(outer, low)
        new_right[down, :] = 0.95 * right_pair[k] + 0.05 * jnp.concatenate(
            [inner[span] for span in parts], axis=1
        )
    for k, q in zip(slots, back):
        result = own_halves(stacked(right_rows[k], beside(q)), low).T
        direction[k * BLOCK : (k + 1) * BLOCK, :] = jnp.concatenate(
            [result[span] for span in parts], axis=1
        )


def reduce_kernel(
    nz, kept, keep_ref, acts_hbm, up_hbm,
    left_gram, right_gram, left_basis, right_basis, moment,
    new_left, new_right, direction,
    acts, up, upt, product, acc, states,
    left_by, left_turned, right_rows, right_turned, moment_turned, left_pair, right_pair,
    send1, send2, send3, recv1, recv2, recv3,
    ssend1, ssend2, ssend3, srecv1, srecv2, srecv3,
    load_sems, state_sems, up_sems, sems1, sems2, sems3,
):
    dp, seq = lax.axis_index("dp"), lax.axis_index("seq")
    x, y, z = lax.rem(dp, 2), lax.rem(dp // 2, 2), dp // 4
    ox, oy = 1 - x, 1 - y
    x_peer = (z * 2 + y) * 2 + ox
    y_peer = (z * 2 + oy) * 2 + x
    first_peer = (x_peer, y_peer)
    second_peer = (y_peer, x_peer)

    def z_target(step):
        turn_z = step // 2
        last = turn_z // max(nz - 1, 1)
        return lax.rem(z + (1 - last) * (lax.rem(turn_z + nz // 2 - 1, max(nz - 1, 1)) + 1), nz)

    def z_peer(step):
        return (z_target(step) * 2 + y) * 2 + x

    width = 4 * LANES

    def load(turn_z):
        columns = pl.ds(pl.multiple_of(z_target(2 * turn_z) * width, width), width)
        return pltpu.make_async_copy(
            acts_hbm.at[:, columns], acts.at[turn_z], load_sems.at[turn_z + 1]
        )

    up_load = pltpu.make_async_copy(up_hbm, up, load_sems.at[0])
    up_load.start()
    for turn_z in range(nz):
        load(turn_z).start()

    state_loads = [
        pltpu.make_async_copy(ref.at[0, 0], states.at[i], state_sems.at[i])
        for i, ref in enumerate((left_gram, right_gram, left_basis, right_basis, moment))
    ]
    for state_load in state_loads:
        state_load.start()
    held = tuple(states.at[i] for i in range(len(state_loads)))
    ready = (
        left_by, left_turned, right_rows, right_turned, moment_turned, left_pair, right_pair,
    )

    barrier = pltpu.get_barrier_semaphore()
    pl.semaphore_signal(barrier, inc=1, device_id=(dp, 1 - seq), device_id_type=MESH)
    for peer in (x_peer, y_peer) + tuple(z_peer(2 * turn_z) for turn_z in range(nz - 1)):
        pl.semaphore_signal(barrier, inc=1, device_id=(peer, seq), device_id_type=MESH)
    up_load.wait()
    upt[seq] = up[...].T
    pl.semaphore_wait(barrier, nz + 2)

    def remote(src, dst, sems, peer):
        return pltpu.make_async_remote_copy(
            src_ref=src, dst_ref=dst, send_sem=sems.at[0], recv_sem=sems.at[1],
            device_id=peer, device_id_type=MESH,
        )

    up_copy = remote(upt.at[seq], upt.at[seq], up_sems, (dp, 1 - seq))
    up_copy.start()
    up_copy.wait()

    half_slots = kept // 2
    run = half_slots // 2
    steps = 2 * nz
    blocks = 8 * nz
    low = lax.broadcasted_iota(jnp.int32, (BLOCK, LANES), 1) < BLOCK

    def copies1(half, step):
        peer = (first_peer[half], seq)
        return (
            remote(send1.at[half, step], recv1.at[half, step], sems1.at[half, step, 0], peer),
            remote(ssend1.at[half, step], srecv1.at[half, step], sems1.at[half, step, 1], peer),
        )

    def copies2(half, step):
        peer = (second_peer[half], seq)
        return (
            remote(send2.at[half, step], recv2.at[half, step], sems2.at[half, step, 0], peer),
            remote(ssend2.at[half, step], srecv2.at[half, step], sems2.at[half, step, 1], peer),
        )

    def copies3(half, step):
        peer = (z_peer(step), seq)
        return (
            remote(send3.at[half, step], recv3.at[half, step], sems3.at[half, step, 0], peer),
            remote(ssend3.at[half, step], srecv3.at[half, step], sems3.at[half, step, 1], peer),
        )

    def multiply(turn_z):
        load(turn_z).wait()
        for dy in (1, 0):
            to_y = y if dy == 0 else oy
            columns = pl.ds(pl.multiple_of(to_y * (2 * LANES), 2 * LANES), 2 * LANES)
            whole = jnp.dot(
                jnp.concatenate([upt[0], upt[1]], axis=1),
                acts[turn_z, :, columns],
                preferred_element_type=jnp.float32,
            )
            product[dy, 0] = whole[:, :LANES].reshape(-1, BLOCK, LANES)
            product[dy, 1] = whole[:, LANES:].reshape(-1, BLOCK, LANES)

    def produce(step):
        for dy in (1, 0):
            to_y = y if dy == 0 else oy
            for dx in (1, 0):
                to_x = x if dx == 0 else ox
                row_block = seq * blocks + ((z_target(step) * 2 + to_y) * 2 + to_x) * 2
                for half in range(2):
                    parts = []
                    for i in range(run):
                        slot = half * half_slots + lax.rem(step, 2) * run + i
                        top = keep_ref[slot, row_block]
                        bottom = keep_ref[slot, row_block + 1]
                        parts.append(
                            jnp.where(low, product[dy, to_x, top], product[dy, to_x, bottom])
                        )
                    value = jnp.concatenate(parts, axis=0)
                    away, place = ((dx, dy), (dy, dx))[half]
                    if away:
                        coded, scale = encode(value)
                        send1[half, step, place] = coded
                        ssend1[half, step, place] = jnp.broadcast_to(scale, (8, LANES))
                    else:
                        acc[half, step, place] = value
            for copy in copies1(dy, step):
                copy.start()

    def forward(step):
        for half in (1, 0):
            for copy in copies1(half, step):
                copy.wait_recv()
            away = acc[half, step, 1] + decode(
                recv1[half, step, 1], srecv1[half, step, 1, 0:1, :]
            )
            coded, scale = encode(away)
            send2[half, step] = coded
            ssend2[half, step] = jnp.broadcast_to(scale, (8, LANES))
            for copy in copies2(half, step):
                copy.start()
            acc[half, step, 0] += decode(recv1[half, step, 0], srecv1[half, step, 0, 0:1, :])

    def settle(step, half):
        for copy in copies2(half, step):
            copy.wait_recv()
        return acc[half, step, 0] + decode(recv2[half, step], srecv2[half, step, 0:1, :])

    def spread(step):
        for half in (1, 0):
            coded, scale = encode(settle(step, half))
            send3[half, step] = coded
            ssend3[half, step] = jnp.broadcast_to(scale, (8, LANES))
            for copy in copies3(half, step):
                copy.start()

    def turn(step, carry):
        @pl.when((step < steps) & (lax.rem(step, 2) == 0))
        def _():
            multiply(step // 2)

        @pl.when(step < steps)
        def _():
            produce(step)

        @pl.when(step == 1)
        def _():
            for state_load in state_loads:
                state_load.wait()

        @pl.when((step >= 1) & (step <= steps))
        def _():
            for i in range(kept // steps):
                prepare((step - 1) * (kept // steps) + i, kept, low, held, ready)

        @pl.when(step >= LAG)
        def _():
            forward(step - LAG)

        @pl.when(step >= 2 * LAG)
        def _():
            spread(step - 2 * LAG)

        return carry

    lax.fori_loop(0, steps + LAG, turn, 0)

    for odd in range(2):
        slots, blocks_done = [], []
        for half in (1, 0):
            total = settle(steps - 2 + odd, half)
            for step in range(odd, steps - 2, 2):
                for copy in copies3(half, step):
                    copy.wait_recv()
                total += decode(recv3[half, step], srecv3[half, step, 0:1, :])
            for i in range(run):
                slots.append(half * half_slots + odd * run + i)
                blocks_done.append(total[i * BLOCK : (i + 1) * BLOCK])
        update(slots, blocks_done, low, ready, (new_left, new_right, direction))

    for half in range(2):
        for step in range(steps):
            for copy in copies1(half, step) + copies2(half, step):
                copy.wait_send()
            if step < steps - 2:
                for copy in copies3(half, step):
                    copy.wait_send()


def fused_step(acts, upstream, keep_lists, states, nz):
    kept = keep_lists.shape[1]
    tokens, rows = upstream.shape[0], upstream.shape[1]
    steps = 2 * nz
    rest = max(steps - 2, 1)
    half = (kept // 4 * BLOCK, LANES)
    scale = (8, LANES)
    dma = pltpu.SemaphoreType.DMA
    vmem, hbm = (pl.BlockSpec(memory_space=space) for space in (pltpu.VMEM, pltpu.HBM))
    return pl.pallas_call(
        functools.partial(reduce_kernel, nz, kept),
        out_shape=(jax.ShapeDtypeStruct((kept * BLOCK, LANES), jnp.float32),) * 3,
        in_specs=[pl.BlockSpec(memory_space=pltpu.SMEM)] + [hbm] * (2 + len(states)),
        out_specs=(vmem,) * 3,
        scratch_shapes=[
            pltpu.VMEM((nz, acts.shape[0], 4 * LANES), jnp.bfloat16),
            pltpu.VMEM(upstream.shape, jnp.bfloat16),
            pltpu.VMEM((2, rows, tokens), jnp.bfloat16),
            pltpu.VMEM((2, 2, rows // BLOCK, BLOCK, LANES), jnp.float32),
            pltpu.VMEM((2, steps, 2) + half, jnp.float32),
            pltpu.VMEM((len(states),) + states[0].shape[2:], jnp.float32),
            pltpu.VMEM((kept, LANES, 2 * LANES), jnp.bfloat16),
            pltpu.VMEM((kept, LANES, 2 * LANES), jnp.bfloat16),
            pltpu.VMEM((kept, 2 * LANES, BLOCK), jnp.bfloat16),
            pltpu.VMEM((kept, 2 * LANES, BLOCK), jnp.bfloat16),
            pltpu.VMEM((kept, BLOCK, LANES), jnp.float32),
            pltpu.VMEM((kept, BLOCK, LANES), jnp.float32),
            pltpu.VMEM((kept, BLOCK, LANES), jnp.float32),
            pltpu.VMEM((2, steps, 2) + half, jnp.int16),
            pltpu.VMEM((2, steps) + half, jnp.int16),
            pltpu.VMEM((2, rest) + half, jnp.int16),
            pltpu.VMEM((2, steps, 2) + half, jnp.int16),
            pltpu.VMEM((2, steps) + half, jnp.int16),
            pltpu.VMEM((2, rest) + half, jnp.int16),
            pltpu.VMEM((2, steps, 2) + scale, jnp.float32),
            pltpu.VMEM((2, steps) + scale, jnp.float32),
            pltpu.VMEM((2, rest) + scale, jnp.float32),
            pltpu.VMEM((2, steps, 2) + scale, jnp.float32),
            pltpu.VMEM((2, steps) + scale, jnp.float32),
            pltpu.VMEM((2, rest) + scale, jnp.float32),
            dma((nz + 1,)),
            dma((len(states),)),
            dma((2,)),
            dma((2, steps, 2, 2)),
            dma((2, steps, 2, 2)),
            dma((2, rest, 2, 2)),
        ],
        compiler_params=pltpu.CompilerParams(
            collective_id=0, has_side_effects=True, vmem_limit_bytes=GRANT
        ),
        cost_estimate=pl.CostEstimate(
            flops=2 * acts.size * rows,
            bytes_accessed=16 * (acts.size + upstream.size),
            transcendentals=0,
        ),
        name="fused_step",
    )(keep_lists.T, acts, upstream, *states)


def unpair_kernel(kept, *refs):
    count = (len(refs) - 2) // 2
    staged, sems = refs[-2:]
    copies = [
        pltpu.make_async_copy(staged.at[i], refs[count + i].at[0, 0], sems.at[i])
        for i in range(count)
    ]
    for i in range(count):
        for slot in range(kept):
            pair = refs[i][slot * BLOCK : (slot + 1) * BLOCK, :]
            staged[i, slot] = pair[:, :BLOCK]
            staged[i, kept + slot] = pair[:, BLOCK:]
        copies[i].start()
    for copy in copies:
        copy.wait()


def unpaired(arrays, shape):
    vmem, hbm = (pl.BlockSpec(memory_space=space) for space in (pltpu.VMEM, pltpu.HBM))
    count = len(arrays)
    return pl.pallas_call(
        functools.partial(unpair_kernel, arrays[0].shape[0] // BLOCK),
        out_shape=(jax.ShapeDtypeStruct(shape, jnp.float32),) * count,
        in_specs=[vmem] * count,
        out_specs=(hbm,) * count,
        scratch_shapes=[
            pltpu.VMEM((count,) + shape[2:], jnp.float32),
            pltpu.SemaphoreType.DMA((count,)),
        ],
        compiler_params=pltpu.CompilerParams(vmem_limit_bytes=GRANT),
        name="unpair",
    )(*arrays)


def per_device(
    acts, upstream, keep_lists, left_gram, right_gram, left_basis, right_basis, second_moment
):
    share_rows = acts.shape[1]
    share_blocks = share_rows // BLOCK
    kept = keep_lists.shape[1]
    data_size = lax.axis_size("dp")
    fits = (
        lax.axis_size("seq") == 2
        and data_size % 4 == 0
        and share_rows == data_size * LANES
        and kept % (data_size // 2) == 0
        and kept % 4 == 0
        and upstream.shape[0] % LANES == 0
    )
    if fits:
        states = (left_gram, right_gram, left_basis, right_basis, second_moment)
        pairs = fused_step(acts, upstream, keep_lists, states, data_size // 4)
        return unpaired(pairs, left_gram.shape)
    else:
        kept_share = lax.dynamic_slice_in_dim(
            keep_lists, lax.axis_index("seq") * share_blocks, share_blocks, 0
        )
        gathered = lax.all_gather(upstream, "seq", axis=0, tiled=True)
        grad = lax.dot_general(
            acts, gathered, (((0,), (0,)), ((), ())), preferred_element_type=jnp.float32
        )
        tiles = grad.reshape(share_blocks, BLOCK, grad.shape[1] // BLOCK, BLOCK)
        picked = jnp.take_along_axis(tiles, kept_share[:, None, :, None], axis=2)
        outgoing = picked.transpose(0, 2, 1, 3).reshape(data_size, -1, BLOCK * BLOCK)
        owned_sum = lax.psum_scatter(outgoing, "dp", scatter_dimension=0)
        gradient = owned_sum.reshape(1, 1, -1, BLOCK, BLOCK)
    return precondition(
        gradient, left_gram, right_gram, left_basis, right_basis, second_moment
    )


def solution(mesh):
    block = P("seq", "dp", None, None, None)
    return jax.shard_map(
        per_device,
        mesh=mesh,
        in_specs=(P("dp", "seq"), P(("dp", "seq"), None), P()) + (block,) * 5,
        out_specs=(block,) * 3,
        check_vma=False,
    )
```

```python
import functools

import jax
import jax.numpy as jnp
from jax import lax
from jax.experimental import pallas as pl
from jax.experimental.pallas import tpu as pltpu
from jax.sharding import PartitionSpec as P

BLOCK = 64
LANES = 128
TOP = 32766.0
GRANT = 65000 * 1024
LAG = 2
MESH = pl.DeviceIdType.MESH


def precondition(gradient, left_gram, right_gram, left_basis, right_basis, second_moment):
    highest = lax.Precision.HIGHEST
    new_left = 0.95 * left_gram + 0.05 * jnp.einsum(
        "...ij,...kj->...ik", gradient, gradient, precision=highest
    )
    new_right = 0.95 * right_gram + 0.05 * jnp.einsum(
        "...ji,...jk->...ik", gradient, gradient, precision=highest
    )
    partial_rot = jnp.einsum("...ji,...jk->...ik", left_basis, gradient, precision=highest)
    rotated = jnp.einsum("...ij,...jk->...ik", partial_rot, right_basis, precision=highest)
    second = 0.95 * second_moment + 0.05 * rotated * rotated
    scaled = rotated / (jnp.sqrt(second) + 1e-08)
    partial_back = jnp.einsum("...ij,...jk->...ik", left_basis, scaled, precision=highest)
    direction = jnp.einsum("...ij,...kj->...ik", partial_back, right_basis, precision=highest)
    return (new_left, new_right, direction)


def encode(value):
    peak = jnp.maximum(jnp.max(jnp.abs(value), axis=0, keepdims=True), 1e-30)
    coded = jnp.round(value * (TOP / peak)).astype(jnp.int32).astype(jnp.int16)
    return coded, peak * (1.0 / TOP)


def decode(coded, scale):
    return coded.astype(jnp.int32).astype(jnp.float32) * scale


def split(value):
    high = value.astype(jnp.bfloat16)
    return high, (value - high.astype(jnp.float32)).astype(jnp.bfloat16)


def stacked(left, right):
    out = jnp.dot(left, right, preferred_element_type=jnp.float32)
    rows, columns = out.shape[0] // 2, out.shape[1] // 2
    return out[:rows, :columns] + (out[:rows, columns:] + out[rows:, :columns])


def rows_of(value):
    return jnp.concatenate(split(value), axis=0)


def beside(value):
    return jnp.concatenate(split(value), axis=1)


def diagonal(pair, low):
    return jnp.concatenate([jnp.where(low, pair, 0.0), jnp.where(low, 0.0, pair)], axis=0)


def own_halves(value, low):
    return jnp.where(low, value[:BLOCK], value[BLOCK:])


def prepare(slot, kept, low, states, ready):
    left_gram, right_gram, left_basis, right_basis, moment = states
    left_by, left_turned, right_rows, right_turned, moment_turned, left_pair, right_pair = ready
    pair = (slot, kept + slot)
    left = jnp.concatenate([left_basis[at] for at in pair], axis=1)
    left_by[slot] = beside(diagonal(left, low))
    left_t = jnp.concatenate([left_basis[at].T for at in pair], axis=1)
    left_turned[slot] = beside(diagonal(left_t, low))
    right_rows[slot] = rows_of(jnp.concatenate([right_basis[at] for at in pair], axis=0))
    right_turned[slot] = rows_of(jnp.concatenate([right_basis[at].T for at in pair], axis=0))
    moment_turned[slot] = jnp.concatenate([moment[at].T for at in pair], axis=1)
    left_pair[slot] = jnp.concatenate([left_gram[at] for at in pair], axis=1)
    right_pair[slot] = jnp.concatenate([right_gram[at] for at in pair], axis=1)


def update(slots, blocks, low, ready, outs):
    left_by, left_turned, right_rows, right_turned, moment_turned, left_pair, right_pair = ready
    new_left, new_right, direction = outs
    parts = (slice(0, BLOCK), slice(BLOCK, LANES))
    partial = [stacked(rows_of(t), left_by[k]) for k, t in zip(slots, blocks)]
    turned = [t.T for t in blocks]
    rotated = [
        own_halves(stacked(right_turned[k], beside(p)), low) for k, p in zip(slots, partial)
    ]
    scaled = [
        r / (jnp.sqrt(0.95 * moment_turned[k] + 0.05 * r * r) + 1e-08)
        for k, r in zip(slots, rotated)
    ]
    back = [stacked(rows_of(v), left_turned[k]) for k, v in zip(slots, scaled)]
    for k, t, u in zip(slots, blocks, turned):
        outer = stacked(rows_of(u), beside(t))
        masked = split(jnp.concatenate([jnp.where(low, t, 0.0), jnp.where(low, 0.0, t)], axis=0))
        halves = split(u)
        dot = functools.partial(jnp.dot, preferred_element_type=jnp.float32)
        inner = dot(masked[0], halves[0]) + (
            dot(masked[0], halves[1]) + dot(masked[1], halves[0])
        )
        down = slice(k * BLOCK, (k + 1) * BLOCK)
        new_left[down, :] = 0.95 * left_pair[k] + 0.05 * own_halves(outer, low)
        new_right[down, :] = 0.95 * right_pair[k] + 0.05 * jnp.concatenate(
            [inner[span] for span in parts], axis=1
        )
    for k, q in zip(slots, back):
        result = own_halves(stacked(right_rows[k], beside(q)), low).T
        direction[k * BLOCK : (k + 1) * BLOCK, :] = jnp.concatenate(
            [result[span] for span in parts], axis=1
        )


def reduce_kernel(
    nz, kept, keep_ref, acts_hbm, up_hbm,
    left_gram, right_gram, left_basis, right_basis, moment,
    new_left, new_right, direction,
    acts, up, upt, product, acc, states,
    left_by, left_turned, right_rows, right_turned, moment_turned, left_pair, right_pair,
    send1, send2, send3, recv1, recv2, recv3,
    ssend1, ssend2, ssend3, srecv1, srecv2, srecv3,
    load_sems, state_sems, up_sems, sems1, sems2, sems3,
):
    dp, seq = lax.axis_index("dp"), lax.axis_index("seq")
    x, y, z = lax.rem(dp, 2), lax.rem(dp // 2, 2), dp // 4
    ox, oy = 1 - x, 1 - y
    x_peer = (z * 2 + y) * 2 + ox
    y_peer = (z * 2 + oy) * 2 + x
    first_peer = (x_peer, y_peer)
    second_peer = (y_peer, x_peer)

    def z_target(step):
        turn_z = step // 2
        last = turn_z // max(nz - 1, 1)
        return lax.rem(z + (1 - last) * (lax.rem(turn_z + nz // 2 - 1, max(nz - 1, 1)) + 1), nz)

    def z_peer(step):
        return (z_target(step) * 2 + y) * 2 + x

    width = 4 * LANES

    def load(turn_z):
        columns = pl.ds(pl.multiple_of(z_target(2 * turn_z) * width, width), width)
        return pltpu.make_async_copy(
            acts_hbm.at[:, columns], acts.at[turn_z], load_sems.at[turn_z + 1]
        )

    up_load = pltpu.make_async_copy(up_hbm, up.at[seq], load_sems.at[0])
    up_load.start()
    for turn_z in range(nz):
        load(turn_z).start()

    state_loads = [
        pltpu.make_async_copy(ref.at[0, 0], states.at[i], state_sems.at[i])
        for i, ref in enumerate((left_gram, right_gram, left_basis, right_basis, moment))
    ]
    for state_load in state_loads:
        state_load.start()
    held = tuple(states.at[i] for i in range(len(state_loads)))
    ready = (
        left_by, left_turned, right_rows, right_turned, moment_turned, left_pair, right_pair,
    )

    barrier = pltpu.get_barrier_semaphore()
    pl.semaphore_signal(barrier, inc=1, device_id=(dp, 1 - seq), device_id_type=MESH)
    for peer in (x_peer, y_peer) + tuple(z_peer(2 * turn_z) for turn_z in range(nz - 1)):
        pl.semaphore_signal(barrier, inc=1, device_id=(peer, seq), device_id_type=MESH)
    pl.semaphore_wait(barrier, nz + 2)

    def remote(src, dst, sems, peer):
        return pltpu.make_async_remote_copy(
            src_ref=src, dst_ref=dst, send_sem=sems.at[0], recv_sem=sems.at[1],
            device_id=peer, device_id_type=MESH,
        )

    up_copy = remote(up_hbm, up.at[seq], up_sems, (dp, 1 - seq))
    up_copy.start()
    up_load.wait()
    upt[seq] = up[seq].T
    up_copy.wait()
    upt[1 - seq] = up[1 - seq].T

    half_slots = kept // 2
    run = half_slots // 2
    steps = 2 * nz
    blocks = 8 * nz
    low = lax.broadcasted_iota(jnp.int32, (BLOCK, LANES), 1) < BLOCK

    def copies1(half, step):
        peer = (first_peer[half], seq)
        return (
            remote(send1.at[half, step], recv1.at[half, step], sems1.at[half, step, 0], peer),
            remote(ssend1.at[half, step], srecv1.at[half, step], sems1.at[half, step, 1], peer),
        )

    def copies2(half, step):
        peer = (second_peer[half], seq)
        return (
            remote(send2.at[half, step], recv2.at[half, step], sems2.at[half, step, 0], peer),
            remote(ssend2.at[half, step], srecv2.at[half, step], sems2.at[half, step, 1], peer),
        )

    def copies3(half, step):
        peer = (z_peer(step), seq)
        return (
            remote(send3.at[half, step], recv3.at[half, step], sems3.at[half, step, 0], peer),
            remote(ssend3.at[half, step], srecv3.at[half, step], sems3.at[half, step, 1], peer),
        )

    def multiply(turn_z, dy):
        to_y = y if dy == 0 else oy
        columns = pl.ds(pl.multiple_of(to_y * (2 * LANES), 2 * LANES), 2 * LANES)
        whole = jnp.dot(
            jnp.concatenate([upt[0], upt[1]], axis=1),
            acts[turn_z, :, columns],
            preferred_element_type=jnp.float32,
        )
        product[dy, 0] = whole[:, :LANES].reshape(-1, BLOCK, LANES)
        product[dy, 1] = whole[:, LANES:].reshape(-1, BLOCK, LANES)

    def produce(step, dy):
        to_y = y if dy == 0 else oy
        for dx in (1, 0):
            to_x = x if dx == 0 else ox
            row_block = seq * blocks + ((z_target(step) * 2 + to_y) * 2 + to_x) * 2
            for half in range(2):
                parts = []
                for i in range(run):
                    slot = half * half_slots + lax.rem(step, 2) * run + i
                    top = keep_ref[slot, row_block]
                    bottom = keep_ref[slot, row_block + 1]
                    parts.append(
                        jnp.where(low, product[dy, to_x, top], product[dy, to_x, bottom])
                    )
                value = jnp.concatenate(parts, axis=0)
                away, place = ((dx, dy), (dy, dx))[half]
                if away:
                    coded, scale = encode(value)
                    send1[half, step, place] = coded
                    ssend1[half, step, place] = jnp.broadcast_to(scale, (8, LANES))
                else:
                    acc[half, step, place] = value
        for copy in copies1(dy, step):
            copy.start()

    def forward(step):
        for half in (1, 0):
            for copy in copies1(half, step):
                copy.wait_recv()
            away = acc[half, step, 1] + decode(
                recv1[half, step, 1], srecv1[half, step, 1, 0:1, :]
            )
            coded, scale = encode(away)
            send2[half, step] = coded
            ssend2[half, step] = jnp.broadcast_to(scale, (8, LANES))
            for copy in copies2(half, step):
                copy.start()
            acc[half, step, 0] += decode(recv1[half, step, 0], srecv1[half, step, 0, 0:1, :])

    def settle(step, half):
        for copy in copies2(half, step):
            copy.wait_recv()
        return acc[half, step, 0] + decode(recv2[half, step], srecv2[half, step, 0:1, :])

    def spread(step):
        for half in (1, 0):
            coded, scale = encode(settle(step, half))
            send3[half, step] = coded
            ssend3[half, step] = jnp.broadcast_to(scale, (8, LANES))
            for copy in copies3(half, step):
                copy.start()

    def turn(step, carry):
        @pl.when((step < steps) & (lax.rem(step, 2) == 0))
        def _():
            load(step // 2).wait()
            for dy in (1, 0):
                multiply(step // 2, dy)
                produce(step, dy)

        @pl.when((step < steps) & (lax.rem(step, 2) == 1))
        def _():
            for dy in (1, 0):
                produce(step, dy)

        @pl.when(step == 1)
        def _():
            for state_load in state_loads:
                state_load.wait()

        @pl.when((step >= 1) & (step <= steps))
        def _():
            for i in range(kept // steps):
                prepare((step - 1) * (kept // steps) + i, kept, low, held, ready)

        @pl.when(step >= LAG)
        def _():
            forward(step - LAG)

        @pl.when(step >= 2 * LAG)
        def _():
            spread(step - 2 * LAG)

        return carry

    lax.fori_loop(0, steps + LAG, turn, 0)

    for odd in range(2):
        slots, blocks_done = [], []
        for half in (1, 0):
            total = settle(steps - 2 + odd, half)
            for step in range(odd, steps - 2, 2):
                for copy in copies3(half, step):
                    copy.wait_recv()
                total += decode(recv3[half, step], srecv3[half, step, 0:1, :])
            for i in range(run):
                slots.append(half * half_slots + odd * run + i)
                blocks_done.append(total[i * BLOCK : (i + 1) * BLOCK])
        update(slots, blocks_done, low, ready, (new_left, new_right, direction))

    for half in range(2):
        for step in range(steps):
            for copy in copies1(half, step) + copies2(half, step):
                copy.wait_send()
            if step < steps - 2:
                for copy in copies3(half, step):
                    copy.wait_send()


def fused_step(acts, upstream, keep_lists, states, nz):
    kept = keep_lists.shape[1]
    tokens, rows = upstream.shape[0], upstream.shape[1]
    steps = 2 * nz
    rest = max(steps - 2, 1)
    half = (kept // 4 * BLOCK, LANES)
    scale = (8, LANES)
    dma = pltpu.SemaphoreType.DMA
    vmem, hbm = (pl.BlockSpec(memory_space=space) for space in (pltpu.VMEM, pltpu.HBM))
    return pl.pallas_call(
        functools.partial(reduce_kernel, nz, kept),
        out_shape=(jax.ShapeDtypeStruct((kept * BLOCK, LANES), jnp.float32),) * 3,
        in_specs=[pl.BlockSpec(memory_space=pltpu.SMEM)] + [hbm] * (2 + len(states)),
        out_specs=(vmem,) * 3,
        scratch_shapes=[
            pltpu.VMEM((nz, acts.shape[0], 4 * LANES), jnp.bfloat16),
            pltpu.VMEM((2,) + upstream.shape, jnp.bfloat16),
            pltpu.VMEM((2, rows, tokens), jnp.bfloat16),
            pltpu.VMEM((2, 2, rows // BLOCK, BLOCK, LANES), jnp.float32),
            pltpu.VMEM((2, steps, 2) + half, jnp.float32),
            pltpu.VMEM((len(states),) + states[0].shape[2:], jnp.float32),
            pltpu.VMEM((kept, LANES, 2 * LANES), jnp.bfloat16),
            pltpu.VMEM((kept, LANES, 2 * LANES), jnp.bfloat16),
            pltpu.VMEM((kept, 2 * LANES, BLOCK), jnp.bfloat16),
            pltpu.VMEM((kept, 2 * LANES, BLOCK), jnp.bfloat16),
            pltpu.VMEM((kept, BLOCK, LANES), jnp.float32),
            pltpu.VMEM((kept, BLOCK, LANES), jnp.float32),
            pltpu.VMEM((kept, BLOCK, LANES), jnp.float32),
            pltpu.VMEM((2, steps, 2) + half, jnp.int16),
            pltpu.VMEM((2, steps) + half, jnp.int16),
            pltpu.VMEM((2, rest) + half, jnp.int16),
            pltpu.VMEM((2, steps, 2) + half, jnp.int16),
            pltpu.VMEM((2, steps) + half, jnp.int16),
            pltpu.VMEM((2, rest) + half, jnp.int16),
            pltpu.VMEM((2, steps, 2) + scale, jnp.float32),
            pltpu.VMEM((2, steps) + scale, jnp.float32),
            pltpu.VMEM((2, rest) + scale, jnp.float32),
            pltpu.VMEM((2, steps, 2) + scale, jnp.float32),
            pltpu.VMEM((2, steps) + scale, jnp.float32),
            pltpu.VMEM((2, rest) + scale, jnp.float32),
            dma((nz + 1,)),
            dma((len(states),)),
            dma((2,)),
            dma((2, steps, 2, 2)),
            dma((2, steps, 2, 2)),
            dma((2, rest, 2, 2)),
        ],
        compiler_params=pltpu.CompilerParams(
            collective_id=0, has_side_effects=True, vmem_limit_bytes=GRANT
        ),
        cost_estimate=pl.CostEstimate(
            flops=2 * acts.size * rows,
            bytes_accessed=16 * (acts.size + upstream.size),
            transcendentals=0,
        ),
        name="fused_step",
    )(keep_lists.T, acts, upstream, *states)


def unpair_kernel(kept, *refs):
    count = (len(refs) - 2) // 2
    staged, sems = refs[-2:]
    copies = [
        pltpu.make_async_copy(staged.at[i], refs[count + i].at[0, 0], sems.at[i])
        for i in range(count)
    ]
    for i in range(count):
        for slot in range(kept):
            pair = refs[i][slot * BLOCK : (slot + 1) * BLOCK, :]
            staged[i, slot] = pair[:, :BLOCK]
            staged[i, kept + slot] = pair[:, BLOCK:]
        copies[i].start()
    for copy in copies:
        copy.wait()


def unpaired(arrays, shape):
    vmem, hbm = (pl.BlockSpec(memory_space=space) for space in (pltpu.VMEM, pltpu.HBM))
    count = len(arrays)
    return pl.pallas_call(
        functools.partial(unpair_kernel, arrays[0].shape[0] // BLOCK),
        out_shape=(jax.ShapeDtypeStruct(shape, jnp.float32),) * count,
        in_specs=[vmem] * count,
        out_specs=(hbm,) * count,
        scratch_shapes=[
            pltpu.VMEM((count,) + shape[2:], jnp.float32),
            pltpu.SemaphoreType.DMA((count,)),
        ],
        compiler_params=pltpu.CompilerParams(vmem_limit_bytes=GRANT),
        name="unpair",
    )(*arrays)


def per_device(
    acts, upstream, keep_lists, left_gram, right_gram, left_basis, right_basis, second_moment
):
    share_rows = acts.shape[1]
    share_blocks = share_rows // BLOCK
    kept = keep_lists.shape[1]
    data_size = lax.axis_size("dp")
    fits = (
        lax.axis_size("seq") == 2
        and data_size % 4 == 0
        and share_rows == data_size * LANES
        and kept % (data_size // 2) == 0
        and kept % 4 == 0
        and upstream.shape[0] % LANES == 0
    )
    if fits:
        states = (left_gram, right_gram, left_basis, right_basis, second_moment)
        pairs = fused_step(acts, upstream, keep_lists, states, data_size // 4)
        return unpaired(pairs, left_gram.shape)
    else:
        kept_share = lax.dynamic_slice_in_dim(
            keep_lists, lax.axis_index("seq") * share_blocks, share_blocks, 0
        )
        gathered = lax.all_gather(upstream, "seq", axis=0, tiled=True)
        grad = lax.dot_general(
            acts, gathered, (((0,), (0,)), ((), ())), preferred_element_type=jnp.float32
        )
        tiles = grad.reshape(share_blocks, BLOCK, grad.shape[1] // BLOCK, BLOCK)
        picked = jnp.take_along_axis(tiles, kept_share[:, None, :, None], axis=2)
        outgoing = picked.transpose(0, 2, 1, 3).reshape(data_size, -1, BLOCK * BLOCK)
        owned_sum = lax.psum_scatter(outgoing, "dp", scatter_dimension=0)
        gradient = owned_sum.reshape(1, 1, -1, BLOCK, BLOCK)
    return precondition(
        gradient, left_gram, right_gram, left_basis, right_basis, second_moment
    )


def solution(mesh):
    block = P("seq", "dp", None, None, None)
    return jax.shard_map(
        per_device,
        mesh=mesh,
        in_specs=(P("dp", "seq"), P(("dp", "seq"), None), P()) + (block,) * 5,
        out_specs=(block,) * 3,
        check_vma=False,
    )
```

```python
import functools

import jax
import jax.numpy as jnp
from jax import lax
from jax.experimental import pallas as pl
from jax.experimental.pallas import tpu as pltpu
from jax.sharding import PartitionSpec as P

BLOCK = 64
LANES = 128
TOP = 32766.0
GRANT = 65000 * 1024
LAG = 2
MESH = pl.DeviceIdType.MESH


def precondition(gradient, left_gram, right_gram, left_basis, right_basis, second_moment):
    highest = lax.Precision.HIGHEST
    new_left = 0.95 * left_gram + 0.05 * jnp.einsum(
        "...ij,...kj->...ik", gradient, gradient, precision=highest
    )
    new_right = 0.95 * right_gram + 0.05 * jnp.einsum(
        "...ji,...jk->...ik", gradient, gradient, precision=highest
    )
    partial_rot = jnp.einsum("...ji,...jk->...ik", left_basis, gradient, precision=highest)
    rotated = jnp.einsum("...ij,...jk->...ik", partial_rot, right_basis, precision=highest)
    second = 0.95 * second_moment + 0.05 * rotated * rotated
    scaled = rotated / (jnp.sqrt(second) + 1e-08)
    partial_back = jnp.einsum("...ij,...jk->...ik", left_basis, scaled, precision=highest)
    direction = jnp.einsum("...ij,...kj->...ik", partial_back, right_basis, precision=highest)
    return (new_left, new_right, direction)


def encode(value):
    peak = jnp.maximum(jnp.max(jnp.abs(value), axis=0, keepdims=True), 1e-30)
    coded = jnp.round(value * (TOP / peak)).astype(jnp.int32).astype(jnp.int16)
    return coded, peak * (1.0 / TOP)


def decode(coded, scale):
    return coded.astype(jnp.int32).astype(jnp.float32) * scale


def split(value):
    high = value.astype(jnp.bfloat16)
    return high, (value - high.astype(jnp.float32)).astype(jnp.bfloat16)


def stacked(left, right):
    out = jnp.dot(left, right, preferred_element_type=jnp.float32)
    rows, columns = out.shape[0] // 2, out.shape[1] // 2
    return out[:rows, :columns] + (out[:rows, columns:] + out[rows:, :columns])


def rows_of(value):
    return jnp.concatenate(split(value), axis=0)


def beside(value):
    return jnp.concatenate(split(value), axis=1)


def diagonal(pair, low):
    return jnp.concatenate([jnp.where(low, pair, 0.0), jnp.where(low, 0.0, pair)], axis=0)


def own_halves(value, low):
    return jnp.where(low, value[:BLOCK], value[BLOCK:])


def prepare(slot, kept, low, states, ready):
    left_gram, right_gram, left_basis, right_basis, moment = states
    left_by, left_turned, right_rows, right_turned, moment_turned, left_pair, right_pair = ready
    pair = (slot, kept + slot)
    left = jnp.concatenate([left_basis[at] for at in pair], axis=1)
    left_by[slot] = beside(diagonal(left, low))
    left_t = jnp.concatenate([left_basis[at].T for at in pair], axis=1)
    left_turned[slot] = beside(diagonal(left_t, low))
    right_rows[slot] = rows_of(jnp.concatenate([right_basis[at] for at in pair], axis=0))
    right_turned[slot] = rows_of(jnp.concatenate([right_basis[at].T for at in pair], axis=0))
    moment_turned[slot] = jnp.concatenate([moment[at].T for at in pair], axis=1)
    left_pair[slot] = jnp.concatenate([left_gram[at] for at in pair], axis=1)
    right_pair[slot] = jnp.concatenate([right_gram[at] for at in pair], axis=1)


def update(slots, blocks, low, ready, outs):
    left_by, left_turned, right_rows, right_turned, moment_turned, left_pair, right_pair = ready
    new_left, new_right, direction = outs
    parts = (slice(0, BLOCK), slice(BLOCK, LANES))
    partial = [stacked(rows_of(t), left_by[k]) for k, t in zip(slots, blocks)]
    turned = [t.T for t in blocks]
    rotated = [
        own_halves(stacked(right_turned[k], beside(p)), low) for k, p in zip(slots, partial)
    ]
    scaled = [
        r / (jnp.sqrt(0.95 * moment_turned[k] + 0.05 * r * r) + 1e-08)
        for k, r in zip(slots, rotated)
    ]
    back = [stacked(rows_of(v), left_turned[k]) for k, v in zip(slots, scaled)]
    for k, t, u in zip(slots, blocks, turned):
        outer = stacked(rows_of(u), beside(t))
        masked = split(jnp.concatenate([jnp.where(low, t, 0.0), jnp.where(low, 0.0, t)], axis=0))
        halves = split(u)
        dot = functools.partial(jnp.dot, preferred_element_type=jnp.float32)
        inner = dot(masked[0], halves[0]) + (
            dot(masked[0], halves[1]) + dot(masked[1], halves[0])
        )
        down = slice(k * BLOCK, (k + 1) * BLOCK)
        new_left[down, :] = 0.95 * left_pair[k] + 0.05 * own_halves(outer, low)
        new_right[down, :] = 0.95 * right_pair[k] + 0.05 * jnp.concatenate(
            [inner[span] for span in parts], axis=1
        )
    for k, q in zip(slots, back):
        result = own_halves(stacked(right_rows[k], beside(q)), low).T
        direction[k * BLOCK : (k + 1) * BLOCK, :] = jnp.concatenate(
            [result[span] for span in parts], axis=1
        )


def reduce_kernel(
    nz, kept, keep_ref, acts_hbm, up_hbm,
    left_gram, right_gram, left_basis, right_basis, moment,
    new_left, new_right, direction,
    acts, up, upt, product, acc, states,
    left_by, left_turned, right_rows, right_turned, moment_turned, left_pair, right_pair,
    send1, send2, send3, recv1, recv2, recv3,
    ssend1, ssend2, ssend3, srecv1, srecv2, srecv3,
    load_sems, state_sems, up_sems, sems1, sems2, sems3,
):
    dp, seq = lax.axis_index("dp"), lax.axis_index("seq")
    x, y, z = lax.rem(dp, 2), lax.rem(dp // 2, 2), dp // 4
    ox, oy = 1 - x, 1 - y
    x_peer = (z * 2 + y) * 2 + ox
    y_peer = (z * 2 + oy) * 2 + x
    first_peer = (x_peer, y_peer)
    second_peer = (y_peer, x_peer)

    def z_target(step):
        turn_z = step // 2
        last = turn_z // max(nz - 1, 1)
        return lax.rem(z + (1 - last) * (lax.rem(turn_z + nz // 2 - 1, max(nz - 1, 1)) + 1), nz)

    def z_peer(step):
        return (z_target(step) * 2 + y) * 2 + x

    width = 4 * LANES

    def load(turn_z):
        columns = pl.ds(pl.multiple_of(z_target(2 * turn_z) * width, width), width)
        return pltpu.make_async_copy(
            acts_hbm.at[:, columns], acts.at[turn_z], load_sems.at[turn_z + 1]
        )

    up_load = pltpu.make_async_copy(up_hbm, up, load_sems.at[0])
    up_load.start()
    for turn_z in range(nz):
        load(turn_z).start()

    state_loads = [
        pltpu.make_async_copy(ref.at[0, 0], states.at[i], state_sems.at[i])
        for i, ref in enumerate((left_gram, right_gram, left_basis, right_basis, moment))
    ]
    for state_load in state_loads:
        state_load.start()
    held = tuple(states.at[i] for i in range(len(state_loads)))
    ready = (
        left_by, left_turned, right_rows, right_turned, moment_turned, left_pair, right_pair,
    )

    barrier = pltpu.get_barrier_semaphore()
    pl.semaphore_signal(barrier, inc=1, device_id=(dp, 1 - seq), device_id_type=MESH)
    for peer in (x_peer, y_peer) + tuple(z_peer(2 * turn_z) for turn_z in range(nz - 1)):
        pl.semaphore_signal(barrier, inc=1, device_id=(peer, seq), device_id_type=MESH)
    up_load.wait()
    upt[seq] = up[...].T
    pl.semaphore_wait(barrier, nz + 2)

    def remote(src, dst, sems, peer):
        return pltpu.make_async_remote_copy(
            src_ref=src, dst_ref=dst, send_sem=sems.at[0], recv_sem=sems.at[1],
            device_id=peer, device_id_type=MESH,
        )

    up_copy = remote(upt.at[seq], upt.at[seq], up_sems, (dp, 1 - seq))
    up_copy.start()
    up_copy.wait()

    half_slots = kept // 2
    run = half_slots // 2
    steps = 2 * nz
    blocks = 8 * nz
    low = lax.broadcasted_iota(jnp.int32, (BLOCK, LANES), 1) < BLOCK

    def copies1(half, step):
        peer = (first_peer[half], seq)
        return (
            remote(send1.at[half, step], recv1.at[half, step], sems1.at[half, step, 0], peer),
            remote(ssend1.at[half, step], srecv1.at[half, step], sems1.at[half, step, 1], peer),
        )

    def copies2(half, step):
        peer = (second_peer[half], seq)
        return (
            remote(send2.at[half, step], recv2.at[half, step], sems2.at[half, step, 0], peer),
            remote(ssend2.at[half, step], srecv2.at[half, step], sems2.at[half, step, 1], peer),
        )

    def copies3(half, step):
        peer = (z_peer(step), seq)
        return (
            remote(send3.at[half, step], recv3.at[half, step], sems3.at[half, step, 0], peer),
            remote(ssend3.at[half, step], srecv3.at[half, step], sems3.at[half, step, 1], peer),
        )

    def multiply(turn_z):
        load(turn_z).wait()
        for dy in (1, 0):
            to_y = y if dy == 0 else oy
            columns = pl.ds(pl.multiple_of(to_y * (2 * LANES), 2 * LANES), 2 * LANES)
            whole = jnp.dot(
                jnp.concatenate([upt[0], upt[1]], axis=1),
                acts[turn_z, :, columns],
                preferred_element_type=jnp.float32,
            )
            product[dy, 0] = whole[:, :LANES].reshape(-1, BLOCK, LANES)
            product[dy, 1] = whole[:, LANES:].reshape(-1, BLOCK, LANES)

    def produce(step):
        for dy in (1, 0):
            to_y = y if dy == 0 else oy
            for dx in (1, 0):
                to_x = x if dx == 0 else ox
                row_block = seq * blocks + ((z_target(step) * 2 + to_y) * 2 + to_x) * 2
                for half in range(2):
                    parts = []
                    for i in range(run):
                        slot = half * half_slots + lax.rem(step, 2) * run + i
                        top = keep_ref[slot, row_block]
                        bottom = keep_ref[slot, row_block + 1]
                        parts.append(
                            jnp.where(low, product[dy, to_x, top], product[dy, to_x, bottom])
                        )
                    value = jnp.concatenate(parts, axis=0)
                    away, place = ((dx, dy), (dy, dx))[half]
                    if away:
                        coded, scale = encode(value)
                        send1[half, step, place] = coded
                        ssend1[half, step, place] = jnp.broadcast_to(scale, (8, LANES))
                    else:
                        acc[half, step, place] = value
            for copy in copies1(dy, step):
                copy.start()

    def forward(step):
        for half in (1, 0):
            for copy in copies1(half, step):
                copy.wait_recv()
            away = acc[half, step, 1] + decode(
                recv1[half, step, 1], srecv1[half, step, 1, 0:1, :]
            )
            coded, scale = encode(away)
            send2[half, step] = coded
            ssend2[half, step] = jnp.broadcast_to(scale, (8, LANES))
            for copy in copies2(half, step):
                copy.start()
            acc[half, step, 0] += decode(recv1[half, step, 0], srecv1[half, step, 0, 0:1, :])

    def settle(step, half):
        for copy in copies2(half, step):
            copy.wait_recv()
        return acc[half, step, 0] + decode(recv2[half, step], srecv2[half, step, 0:1, :])

    def spread(step):
        for half in (1, 0):
            coded, scale = encode(settle(step, half))
            send3[half, step] = coded
            ssend3[half, step] = jnp.broadcast_to(scale, (8, LANES))
            for copy in copies3(half, step):
                copy.start()

    def turn(step, carry):
        @pl.when(step >= LAG)
        def _():
            forward(step - LAG)

        @pl.when(step >= 2 * LAG)
        def _():
            spread(step - 2 * LAG)

        @pl.when((step < steps) & (lax.rem(step, 2) == 0))
        def _():
            multiply(step // 2)

        @pl.when(step < steps)
        def _():
            produce(step)

        @pl.when(step == 1)
        def _():
            for state_load in state_loads:
                state_load.wait()

        @pl.when((step >= 1) & (step <= steps))
        def _():
            for i in range(kept // steps):
                prepare((step - 1) * (kept // steps) + i, kept, low, held, ready)

        return carry

    lax.fori_loop(0, steps + LAG, turn, 0)

    for odd in range(2):
        slots, blocks_done = [], []
        for half in (1, 0):
            total = settle(steps - 2 + odd, half)
            for step in range(odd, steps - 2, 2):
                for copy in copies3(half, step):
                    copy.wait_recv()
                total += decode(recv3[half, step], srecv3[half, step, 0:1, :])
            for i in range(run):
                slots.append(half * half_slots + odd * run + i)
                blocks_done.append(total[i * BLOCK : (i + 1) * BLOCK])
        update(slots, blocks_done, low, ready, (new_left, new_right, direction))

    for half in range(2):
        for step in range(steps):
            for copy in copies1(half, step) + copies2(half, step):
                copy.wait_send()
            if step < steps - 2:
                for copy in copies3(half, step):
                    copy.wait_send()


def fused_step(acts, upstream, keep_lists, states, nz):
    kept = keep_lists.shape[1]
    tokens, rows = upstream.shape[0], upstream.shape[1]
    steps = 2 * nz
    rest = max(steps - 2, 1)
    half = (kept // 4 * BLOCK, LANES)
    scale = (8, LANES)
    dma = pltpu.SemaphoreType.DMA
    vmem, hbm = (pl.BlockSpec(memory_space=space) for space in (pltpu.VMEM, pltpu.HBM))
    return pl.pallas_call(
        functools.partial(reduce_kernel, nz, kept),
        out_shape=(jax.ShapeDtypeStruct((kept * BLOCK, LANES), jnp.float32),) * 3,
        in_specs=[pl.BlockSpec(memory_space=pltpu.SMEM)] + [hbm] * (2 + len(states)),
        out_specs=(vmem,) * 3,
        scratch_shapes=[
            pltpu.VMEM((nz, acts.shape[0], 4 * LANES), jnp.bfloat16),
            pltpu.VMEM(upstream.shape, jnp.bfloat16),
            pltpu.VMEM((2, rows, tokens), jnp.bfloat16),
            pltpu.VMEM((2, 2, rows // BLOCK, BLOCK, LANES), jnp.float32),
            pltpu.VMEM((2, steps, 2) + half, jnp.float32),
            pltpu.VMEM((len(states),) + states[0].shape[2:], jnp.float32),
            pltpu.VMEM((kept, LANES, 2 * LANES), jnp.bfloat16),
            pltpu.VMEM((kept, LANES, 2 * LANES), jnp.bfloat16),
            pltpu.VMEM((kept, 2 * LANES, BLOCK), jnp.bfloat16),
            pltpu.VMEM((kept, 2 * LANES, BLOCK), jnp.bfloat16),
            pltpu.VMEM((kept, BLOCK, LANES), jnp.float32),
            pltpu.VMEM((kept, BLOCK, LANES), jnp.float32),
            pltpu.VMEM((kept, BLOCK, LANES), jnp.float32),
            pltpu.VMEM((2, steps, 2) + half, jnp.int16),
            pltpu.VMEM((2, steps) + half, jnp.int16),
            pltpu.VMEM((2, rest) + half, jnp.int16),
            pltpu.VMEM((2, steps, 2) + half, jnp.int16),
            pltpu.VMEM((2, steps) + half, jnp.int16),
            pltpu.VMEM((2, rest) + half, jnp.int16),
            pltpu.VMEM((2, steps, 2) + scale, jnp.float32),
            pltpu.VMEM((2, steps) + scale, jnp.float32),
            pltpu.VMEM((2, rest) + scale, jnp.float32),
            pltpu.VMEM((2, steps, 2) + scale, jnp.float32),
            pltpu.VMEM((2, steps) + scale, jnp.float32),
            pltpu.VMEM((2, rest) + scale, jnp.float32),
            dma((nz + 1,)),
            dma((len(states),)),
            dma((2,)),
            dma((2, steps, 2, 2)),
            dma((2, steps, 2, 2)),
            dma((2, rest, 2, 2)),
        ],
        compiler_params=pltpu.CompilerParams(
            collective_id=0, has_side_effects=True, vmem_limit_bytes=GRANT
        ),
        cost_estimate=pl.CostEstimate(
            flops=2 * acts.size * rows,
            bytes_accessed=16 * (acts.size + upstream.size),
            transcendentals=0,
        ),
        name="fused_step",
    )(keep_lists.T, acts, upstream, *states)


def unpair_kernel(kept, *refs):
    count = (len(refs) - 2) // 2
    staged, sems = refs[-2:]
    copies = [
        pltpu.make_async_copy(staged.at[i], refs[count + i].at[0, 0], sems.at[i])
        for i in range(count)
    ]
    for i in range(count):
        for slot in range(kept):
            pair = refs[i][slot * BLOCK : (slot + 1) * BLOCK, :]
            staged[i, slot] = pair[:, :BLOCK]
            staged[i, kept + slot] = pair[:, BLOCK:]
        copies[i].start()
    for copy in copies:
        copy.wait()


def unpaired(arrays, shape):
    vmem, hbm = (pl.BlockSpec(memory_space=space) for space in (pltpu.VMEM, pltpu.HBM))
    count = len(arrays)
    return pl.pallas_call(
        functools.partial(unpair_kernel, arrays[0].shape[0] // BLOCK),
        out_shape=(jax.ShapeDtypeStruct(shape, jnp.float32),) * count,
        in_specs=[vmem] * count,
        out_specs=(hbm,) * count,
        scratch_shapes=[
            pltpu.VMEM((count,) + shape[2:], jnp.float32),
            pltpu.SemaphoreType.DMA((count,)),
        ],
        compiler_params=pltpu.CompilerParams(vmem_limit_bytes=GRANT),
        name="unpair",
    )(*arrays)


def per_device(
    acts, upstream, keep_lists, left_gram, right_gram, left_basis, right_basis, second_moment
):
    share_rows = acts.shape[1]
    share_blocks = share_rows // BLOCK
    kept = keep_lists.shape[1]
    data_size = lax.axis_size("dp")
    fits = (
        lax.axis_size("seq") == 2
        and data_size % 4 == 0
        and share_rows == data_size * LANES
        and kept % (data_size // 2) == 0
        and kept % 4 == 0
        and upstream.shape[0] % LANES == 0
    )
    if fits:
        states = (left_gram, right_gram, left_basis, right_basis, second_moment)
        pairs = fused_step(acts, upstream, keep_lists, states, data_size // 4)
        return unpaired(pairs, left_gram.shape)
    else:
        kept_share = lax.dynamic_slice_in_dim(
            keep_lists, lax.axis_index("seq") * share_blocks, share_blocks, 0
        )
        gathered = lax.all_gather(upstream, "seq", axis=0, tiled=True)
        grad = lax.dot_general(
            acts, gathered, (((0,), (0,)), ((), ())), preferred_element_type=jnp.float32
        )
        tiles = grad.reshape(share_blocks, BLOCK, grad.shape[1] // BLOCK, BLOCK)
        picked = jnp.take_along_axis(tiles, kept_share[:, None, :, None], axis=2)
        outgoing = picked.transpose(0, 2, 1, 3).reshape(data_size, -1, BLOCK * BLOCK)
        owned_sum = lax.psum_scatter(outgoing, "dp", scatter_dimension=0)
        gradient = owned_sum.reshape(1, 1, -1, BLOCK, BLOCK)
    return precondition(
        gradient, left_gram, right_gram, left_basis, right_basis, second_moment
    )


def solution(mesh):
    block = P("seq", "dp", None, None, None)
    return jax.shard_map(
        per_device,
        mesh=mesh,
        in_specs=(P("dp", "seq"), P(("dp", "seq"), None), P()) + (block,) * 5,
        out_specs=(block,) * 3,
        check_vma=False,
    )
```

```python
import functools

import jax
import jax.numpy as jnp
from jax import lax
from jax.experimental import pallas as pl
from jax.experimental.pallas import tpu as pltpu
from jax.sharding import PartitionSpec as P

BLOCK = 64
LANES = 128
TOP = 32766.0
GRANT = 65000 * 1024
LAG = 2
MESH = pl.DeviceIdType.MESH


def precondition(gradient, left_gram, right_gram, left_basis, right_basis, second_moment):
    highest = lax.Precision.HIGHEST
    new_left = 0.95 * left_gram + 0.05 * jnp.einsum(
        "...ij,...kj->...ik", gradient, gradient, precision=highest
    )
    new_right = 0.95 * right_gram + 0.05 * jnp.einsum(
        "...ji,...jk->...ik", gradient, gradient, precision=highest
    )
    partial_rot = jnp.einsum("...ji,...jk->...ik", left_basis, gradient, precision=highest)
    rotated = jnp.einsum("...ij,...jk->...ik", partial_rot, right_basis, precision=highest)
    second = 0.95 * second_moment + 0.05 * rotated * rotated
    scaled = rotated / (jnp.sqrt(second) + 1e-08)
    partial_back = jnp.einsum("...ij,...jk->...ik", left_basis, scaled, precision=highest)
    direction = jnp.einsum("...ij,...kj->...ik", partial_back, right_basis, precision=highest)
    return (new_left, new_right, direction)


def encode(value):
    peak = jnp.maximum(jnp.max(jnp.abs(value), axis=0, keepdims=True), 1e-30)
    coded = jnp.round(value * (TOP / peak)).astype(jnp.int32).astype(jnp.int16)
    return coded, peak * (1.0 / TOP)


def decode(coded, scale):
    return coded.astype(jnp.int32).astype(jnp.float32) * scale


def split(value):
    high = value.astype(jnp.bfloat16)
    return high, (value - high.astype(jnp.float32)).astype(jnp.bfloat16)


def stacked(left, right):
    out = jnp.dot(left, right, preferred_element_type=jnp.float32)
    rows, columns = out.shape[0] // 2, out.shape[1] // 2
    return out[:rows, :columns] + (out[:rows, columns:] + out[rows:, :columns])


def rows_of(value):
    return jnp.concatenate(split(value), axis=0)


def beside(value):
    return jnp.concatenate(split(value), axis=1)


def diagonal(pair, low):
    return jnp.concatenate([jnp.where(low, pair, 0.0), jnp.where(low, 0.0, pair)], axis=0)


def own_halves(value, low):
    return jnp.where(low, value[:BLOCK], value[BLOCK:])


def prepare(slot, kept, low, states, ready):
    left_gram, right_gram, left_basis, right_basis, moment = states
    left_by, left_turned, right_rows, right_turned, moment_turned, left_pair, right_pair = ready
    pair = (slot, kept + slot)
    left = jnp.concatenate([left_basis[at] for at in pair], axis=1)
    left_by[slot] = beside(diagonal(left, low))
    left_t = jnp.concatenate([left_basis[at].T for at in pair], axis=1)
    left_turned[slot] = beside(diagonal(left_t, low))
    right_rows[slot] = rows_of(jnp.concatenate([right_basis[at] for at in pair], axis=0))
    right_turned[slot] = rows_of(jnp.concatenate([right_basis[at].T for at in pair], axis=0))
    moment_turned[slot] = jnp.concatenate([moment[at].T for at in pair], axis=1)
    left_pair[slot] = jnp.concatenate([left_gram[at] for at in pair], axis=1)
    right_pair[slot] = jnp.concatenate([right_gram[at] for at in pair], axis=1)


def update(slots, blocks, low, ready, outs):
    left_by, left_turned, right_rows, right_turned, moment_turned, left_pair, right_pair = ready
    new_left, new_right, direction = outs
    parts = (slice(0, BLOCK), slice(BLOCK, LANES))
    partial = [stacked(rows_of(t), left_by[k]) for k, t in zip(slots, blocks)]
    turned = [t.T for t in blocks]
    rotated = [
        own_halves(stacked(right_turned[k], beside(p)), low) for k, p in zip(slots, partial)
    ]
    scaled = [
        r / (jnp.sqrt(0.95 * moment_turned[k] + 0.05 * r * r) + 1e-08)
        for k, r in zip(slots, rotated)
    ]
    back = [stacked(rows_of(v), left_turned[k]) for k, v in zip(slots, scaled)]
    for k, t, u in zip(slots, blocks, turned):
        outer = stacked(rows_of(u), beside(t))
        masked = split(jnp.concatenate([jnp.where(low, t, 0.0), jnp.where(low, 0.0, t)], axis=0))
        halves = split(u)
        dot = functools.partial(jnp.dot, preferred_element_type=jnp.float32)
        inner = dot(masked[0], halves[0]) + (
            dot(masked[0], halves[1]) + dot(masked[1], halves[0])
        )
        down = slice(k * BLOCK, (k + 1) * BLOCK)
        new_left[down, :] = 0.95 * left_pair[k] + 0.05 * own_halves(outer, low)
        new_right[down, :] = 0.95 * right_pair[k] + 0.05 * jnp.concatenate(
            [inner[span] for span in parts], axis=1
        )
    for k, q in zip(slots, back):
        result = own_halves(stacked(right_rows[k], beside(q)), low).T
        direction[k * BLOCK : (k + 1) * BLOCK, :] = jnp.concatenate(
            [result[span] for span in parts], axis=1
        )


def reduce_kernel(
    nz, kept, keep_ref, acts_hbm, up_hbm,
    left_gram, right_gram, left_basis, right_basis, moment,
    new_left, new_right, direction,
    acts, up, upt, product, acc, states,
    left_by, left_turned, right_rows, right_turned, moment_turned, left_pair, right_pair,
    send1, send2, send3, recv1, recv2, recv3,
    ssend1, ssend2, ssend3, srecv1, srecv2, srecv3,
    load_sems, state_sems, up_sems, sems1, sems2, sems3,
):
    dp, seq = lax.axis_index("dp"), lax.axis_index("seq")
    x, y, z = lax.rem(dp, 2), lax.rem(dp // 2, 2), dp // 4
    ox, oy = 1 - x, 1 - y
    x_peer = (z * 2 + y) * 2 + ox
    y_peer = (z * 2 + oy) * 2 + x
    first_peer = (x_peer, y_peer)
    second_peer = (y_peer, x_peer)

    def z_target(step):
        turn_z = step // 2
        last = turn_z // max(nz - 1, 1)
        return lax.rem(z + (1 - last) * (lax.rem(turn_z + nz // 2 - 1, max(nz - 1, 1)) + 1), nz)

    def z_peer(step):
        return (z_target(step) * 2 + y) * 2 + x

    width = 4 * LANES

    def load(turn_z):
        columns = pl.ds(pl.multiple_of(z_target(2 * turn_z) * width, width), width)
        return pltpu.make_async_copy(
            acts_hbm.at[:, columns], acts.at[turn_z], load_sems.at[turn_z + 1]
        )

    up_load = pltpu.make_async_copy(up_hbm, up, load_sems.at[0])
    up_load.start()
    for turn_z in range(nz):
        load(turn_z).start()

    state_loads = [
        pltpu.make_async_copy(ref.at[0, 0], states.at[i], state_sems.at[i])
        for i, ref in enumerate((left_gram, right_gram, left_basis, right_basis, moment))
    ]
    for state_load in state_loads:
        state_load.start()
    held = tuple(states.at[i] for i in range(len(state_loads)))
    ready = (
        left_by, left_turned, right_rows, right_turned, moment_turned, left_pair, right_pair,
    )

    barrier = pltpu.get_barrier_semaphore()
    pl.semaphore_signal(barrier, inc=1, device_id=(dp, 1 - seq), device_id_type=MESH)
    for peer in (x_peer, y_peer) + tuple(z_peer(2 * turn_z) for turn_z in range(nz - 1)):
        pl.semaphore_signal(barrier, inc=1, device_id=(peer, seq), device_id_type=MESH)
    up_load.wait()
    upt[seq] = up[...].T
    pl.semaphore_wait(barrier, nz + 2)

    def remote(src, dst, sems, peer):
        return pltpu.make_async_remote_copy(
            src_ref=src, dst_ref=dst, send_sem=sems.at[0], recv_sem=sems.at[1],
            device_id=peer, device_id_type=MESH,
        )

    up_copy = remote(upt.at[seq], upt.at[seq], up_sems, (dp, 1 - seq))
    up_copy.start()
    up_copy.wait()

    half_slots = kept // 2
    run = half_slots // 2
    steps = 2 * nz
    blocks = 8 * nz
    low = lax.broadcasted_iota(jnp.int32, (BLOCK, LANES), 1) < BLOCK

    def copies1(half, step):
        peer = (first_peer[half], seq)
        return (
            remote(send1.at[half, step], recv1.at[half, step], sems1.at[half, step, 0], peer),
            remote(ssend1.at[half, step], srecv1.at[half, step], sems1.at[half, step, 1], peer),
        )

    def copies2(half, step):
        peer = (second_peer[half], seq)
        return (
            remote(send2.at[half, step], recv2.at[half, step], sems2.at[half, step, 0], peer),
            remote(ssend2.at[half, step], srecv2.at[half, step], sems2.at[half, step, 1], peer),
        )

    def copies3(half, step):
        peer = (z_peer(step), seq)
        return (
            remote(send3.at[half, step], recv3.at[half, step], sems3.at[half, step, 0], peer),
            remote(ssend3.at[half, step], srecv3.at[half, step], sems3.at[half, step, 1], peer),
        )

    def multiply(turn_z):
        load(turn_z).wait()
        for dy in (1, 0):
            to_y = y if dy == 0 else oy
            columns = pl.ds(pl.multiple_of(to_y * (2 * LANES), 2 * LANES), 2 * LANES)
            whole = jnp.dot(
                jnp.concatenate([upt[0], upt[1]], axis=1),
                acts[turn_z, :, columns],
                preferred_element_type=jnp.float32,
            )
            product[dy, 0] = whole[:, :LANES].reshape(-1, BLOCK, LANES)
            product[dy, 1] = whole[:, LANES:].reshape(-1, BLOCK, LANES)

    def produce(step):
        for dy in (1, 0):
            to_y = y if dy == 0 else oy
            for dx in (1, 0):
                to_x = x if dx == 0 else ox
                row_block = seq * blocks + ((z_target(step) * 2 + to_y) * 2 + to_x) * 2
                for half in range(2):
                    parts = []
                    for i in range(run):
                        slot = half * half_slots + lax.rem(step, 2) * run + i
                        top = keep_ref[slot, row_block]
                        bottom = keep_ref[slot, row_block + 1]
                        parts.append(
                            jnp.where(low, product[dy, to_x, top], product[dy, to_x, bottom])
                        )
                    value = jnp.concatenate(parts, axis=0)
                    away, place = ((dx, dy), (dy, dx))[half]
                    if away:
                        coded, scale = encode(value)
                        send1[half, step, place] = coded
                        ssend1[half, step, place] = jnp.broadcast_to(scale, (8, LANES))
                    else:
                        acc[half, step, place] = value
            for copy in copies1(dy, step):
                copy.start()

    def forward(step):
        for half in (1, 0):
            for copy in copies1(half, step):
                copy.wait_recv()
            away = acc[half, step, 1] + decode(
                recv1[half, step, 1], srecv1[half, step, 1, 0:1, :]
            )
            coded, scale = encode(away)
            send2[half, step] = coded
            ssend2[half, step] = jnp.broadcast_to(scale, (8, LANES))
            for copy in copies2(half, step):
                copy.start()
            acc[half, step, 0] += decode(recv1[half, step, 0], srecv1[half, step, 0, 0:1, :])

    def settle(step, half):
        for copy in copies2(half, step):
            copy.wait_recv()
        return acc[half, step, 0] + decode(recv2[half, step], srecv2[half, step, 0:1, :])

    def spread(step):
        for half in (1, 0):
            coded, scale = encode(settle(step, half))
            send3[half, step] = coded
            ssend3[half, step] = jnp.broadcast_to(scale, (8, LANES))
            for copy in copies3(half, step):
                copy.start()

    def turn(step, carry):
        @pl.when((step < steps) & (lax.rem(step, 2) == 0))
        def _():
            multiply(step // 2)

        @pl.when(step < steps)
        def _():
            produce(step)

        @pl.when(step == 1)
        def _():
            for state_load in state_loads:
                state_load.wait()

        @pl.when((step >= 1) & (step <= steps))
        def _():
            for i in range(kept // steps):
                prepare((step - 1) * (kept // steps) + i, kept, low, held, ready)

        @pl.when(step >= LAG)
        def _():
            forward(step - LAG)

        @pl.when((step > LAG) & (step <= steps))
        def _():
            spread(step - LAG - 1)

        return carry

    lax.fori_loop(0, steps + LAG, turn, 0)

    for odd in range(2):
        slots, blocks_done = [], []
        for half in (1, 0):
            total = settle(steps - 2 + odd, half)
            for step in range(odd, steps - 2, 2):
                for copy in copies3(half, step):
                    copy.wait_recv()
                total += decode(recv3[half, step], srecv3[half, step, 0:1, :])
            for i in range(run):
                slots.append(half * half_slots + odd * run + i)
                blocks_done.append(total[i * BLOCK : (i + 1) * BLOCK])
        update(slots, blocks_done, low, ready, (new_left, new_right, direction))

    for half in range(2):
        for step in range(steps):
            for copy in copies1(half, step) + copies2(half, step):
                copy.wait_send()
            if step < steps - 2:
                for copy in copies3(half, step):
                    copy.wait_send()


def fused_step(acts, upstream, keep_lists, states, nz):
    kept = keep_lists.shape[1]
    tokens, rows = upstream.shape[0], upstream.shape[1]
    steps = 2 * nz
    rest = max(steps - 2, 1)
    half = (kept // 4 * BLOCK, LANES)
    scale = (8, LANES)
    dma = pltpu.SemaphoreType.DMA
    vmem, hbm = (pl.BlockSpec(memory_space=space) for space in (pltpu.VMEM, pltpu.HBM))
    return pl.pallas_call(
        functools.partial(reduce_kernel, nz, kept),
        out_shape=(jax.ShapeDtypeStruct((kept * BLOCK, LANES), jnp.float32),) * 3,
        in_specs=[pl.BlockSpec(memory_space=pltpu.SMEM)] + [hbm] * (2 + len(states)),
        out_specs=(vmem,) * 3,
        scratch_shapes=[
            pltpu.VMEM((nz, acts.shape[0], 4 * LANES), jnp.bfloat16),
            pltpu.VMEM(upstream.shape, jnp.bfloat16),
            pltpu.VMEM((2, rows, tokens), jnp.bfloat16),
            pltpu.VMEM((2, 2, rows // BLOCK, BLOCK, LANES), jnp.float32),
            pltpu.VMEM((2, steps, 2) + half, jnp.float32),
            pltpu.VMEM((len(states),) + states[0].shape[2:], jnp.float32),
            pltpu.VMEM((kept, LANES, 2 * LANES), jnp.bfloat16),
            pltpu.VMEM((kept, LANES, 2 * LANES), jnp.bfloat16),
            pltpu.VMEM((kept, 2 * LANES, BLOCK), jnp.bfloat16),
            pltpu.VMEM((kept, 2 * LANES, BLOCK), jnp.bfloat16),
            pltpu.VMEM((kept, BLOCK, LANES), jnp.float32),
            pltpu.VMEM((kept, BLOCK, LANES), jnp.float32),
            pltpu.VMEM((kept, BLOCK, LANES), jnp.float32),
            pltpu.VMEM((2, steps, 2) + half, jnp.int16),
            pltpu.VMEM((2, steps) + half, jnp.int16),
            pltpu.VMEM((2, rest) + half, jnp.int16),
            pltpu.VMEM((2, steps, 2) + half, jnp.int16),
            pltpu.VMEM((2, steps) + half, jnp.int16),
            pltpu.VMEM((2, rest) + half, jnp.int16),
            pltpu.VMEM((2, steps, 2) + scale, jnp.float32),
            pltpu.VMEM((2, steps) + scale, jnp.float32),
            pltpu.VMEM((2, rest) + scale, jnp.float32),
            pltpu.VMEM((2, steps, 2) + scale, jnp.float32),
            pltpu.VMEM((2, steps) + scale, jnp.float32),
            pltpu.VMEM((2, rest) + scale, jnp.float32),
            dma((nz + 1,)),
            dma((len(states),)),
            dma((2,)),
            dma((2, steps, 2, 2)),
            dma((2, steps, 2, 2)),
            dma((2, rest, 2, 2)),
        ],
        compiler_params=pltpu.CompilerParams(
            collective_id=0, has_side_effects=True, vmem_limit_bytes=GRANT
        ),
        cost_estimate=pl.CostEstimate(
            flops=2 * acts.size * rows,
            bytes_accessed=16 * (acts.size + upstream.size),
            transcendentals=0,
        ),
        name="fused_step",
    )(keep_lists.T, acts, upstream, *states)


def unpair_kernel(kept, *refs):
    count = (len(refs) - 2) // 2
    staged, sems = refs[-2:]
    copies = [
        pltpu.make_async_copy(staged.at[i], refs[count + i].at[0, 0], sems.at[i])
        for i in range(count)
    ]
    for i in range(count):
        for slot in range(kept):
            pair = refs[i][slot * BLOCK : (slot + 1) * BLOCK, :]
            staged[i, slot] = pair[:, :BLOCK]
            staged[i, kept + slot] = pair[:, BLOCK:]
        copies[i].start()
    for copy in copies:
        copy.wait()


def unpaired(arrays, shape):
    vmem, hbm = (pl.BlockSpec(memory_space=space) for space in (pltpu.VMEM, pltpu.HBM))
    count = len(arrays)
    return pl.pallas_call(
        functools.partial(unpair_kernel, arrays[0].shape[0] // BLOCK),
        out_shape=(jax.ShapeDtypeStruct(shape, jnp.float32),) * count,
        in_specs=[vmem] * count,
        out_specs=(hbm,) * count,
        scratch_shapes=[
            pltpu.VMEM((count,) + shape[2:], jnp.float32),
            pltpu.SemaphoreType.DMA((count,)),
        ],
        compiler_params=pltpu.CompilerParams(vmem_limit_bytes=GRANT),
        name="unpair",
    )(*arrays)


def per_device(
    acts, upstream, keep_lists, left_gram, right_gram, left_basis, right_basis, second_moment
):
    share_rows = acts.shape[1]
    share_blocks = share_rows // BLOCK
    kept = keep_lists.shape[1]
    data_size = lax.axis_size("dp")
    fits = (
        lax.axis_size("seq") == 2
        and data_size % 4 == 0
        and share_rows == data_size * LANES
        and kept % (data_size // 2) == 0
        and kept % 4 == 0
        and upstream.shape[0] % LANES == 0
    )
    if fits:
        states = (left_gram, right_gram, left_basis, right_basis, second_moment)
        pairs = fused_step(acts, upstream, keep_lists, states, data_size // 4)
        return unpaired(pairs, left_gram.shape)
    else:
        kept_share = lax.dynamic_slice_in_dim(
            keep_lists, lax.axis_index("seq") * share_blocks, share_blocks, 0
        )
        gathered = lax.all_gather(upstream, "seq", axis=0, tiled=True)
        grad = lax.dot_general(
            acts, gathered, (((0,), (0,)), ((), ())), preferred_element_type=jnp.float32
        )
        tiles = grad.reshape(share_blocks, BLOCK, grad.shape[1] // BLOCK, BLOCK)
        picked = jnp.take_along_axis(tiles, kept_share[:, None, :, None], axis=2)
        outgoing = picked.transpose(0, 2, 1, 3).reshape(data_size, -1, BLOCK * BLOCK)
        owned_sum = lax.psum_scatter(outgoing, "dp", scatter_dimension=0)
        gradient = owned_sum.reshape(1, 1, -1, BLOCK, BLOCK)
    return precondition(
        gradient, left_gram, right_gram, left_basis, right_basis, second_moment
    )


def solution(mesh):
    block = P("seq", "dp", None, None, None)
    return jax.shard_map(
        per_device,
        mesh=mesh,
        in_specs=(P("dp", "seq"), P(("dp", "seq"), None), P()) + (block,) * 5,
        out_specs=(block,) * 3,
        check_vma=False,
    )
```
